128 devices in a mesh: tm: 32 (over x, y, core), space: 2 (over z_hi), clip: 2 (over z_lo).
Axes of the slice: x: 4, y: 4, z: 4 (z_hi: 2, z_lo: 2; z = z_hi * 2 + z_lo), core: 2. Of those that a mesh axis runs over, the one named last changes fastest.
Arguments:
- video: bfloat16 [2, 128, 8, 10240], P('clip', 'tm', 'space'), may hold values from -35 to 35
- conv_first: bfloat16 [1728, 64], replicated, may hold values from -0.15625 to 0.15625
- conv_second: bfloat16 [1728, 64], replicated, may hold values from -0.15625 to 0.15625
- conv_down: bfloat16 [1728, 128], replicated, may hold values from -0.15625 to 0.15625
- down_cotangent: bfloat16 [2, 128, 4, 10240], P('clip', 'tm', 'space'), may hold values from -6 to 6
Outputs:
- down_features: bfloat16 [2, 128, 4, 10240], P('clip', 'tm', 'space')
- grad_video: float32 [2, 128, 8, 10240], P('clip', 'tm', 'space')
- grad_first: float32 [1728, 64], replicated
- grad_second: float32 [1728, 64], replicated
- grad_down: float32 [1728, 128], replicated
The draws below stay inside these ranges and needn't reach their ends.
All inputs are finite; a program needn't handle non-finite values.
Results may differ from the reference program's by a relative error of at most 0.0082.
Values may be sent and summed in bfloat16 or wider, within the bound.
A program may use at most 128 MiB of HBM per device.

```python
import math
import jax
import jax.numpy as jnp
from jax import lax

C = 64
C_OUT = 128
GROUPS = 32
COLS = 160
FRAMES = 128
ROWS = 8
CLIPS = 2
N_CLIP = 2


def draw_video(key, part):
    key = jax.random.fold_in(key, 7)
    noise_key, frame_key, channel_key = jax.random.split(key, 3)
    shape = (CLIPS, FRAMES, ROWS, COLS * C)
    position = jnp.arange(FRAMES, dtype=jnp.float32) / max(FRAMES - 1, 1)
    jitter = jax.random.uniform(frame_key, (CLIPS, FRAMES), minval=-0.1, maxval=0.1)
    channel_level = jax.random.uniform(channel_key, (CLIPS, C), minval=-0.5, maxval=0.5)
    noise = jnp.clip(jax.random.normal(noise_key, shape), -4.0, 4.0)
    tilt = 0.6
    offset = jnp.zeros((CLIPS, C), jnp.float32)
    frame_scale = 10.0 ** (tilt * position[None, :] - tilt / 2 + jitter)
    channel_scale = jnp.tile(10.0 ** channel_level, (1, COLS))
    channel_offset = jnp.tile(offset, (1, COLS))
    values = (noise + channel_offset[:, None, None, :]) * frame_scale[:, :, None, None] * channel_scale[:, None, None, :]
    return values.astype(jnp.bfloat16)


def levels(rng, dims, cuts, smallest, high):
    factor_of, own = 1.0, jax.random.fold_in(rng, 6)
    for dim, parts in cuts:
        heights = jnp.exp(jax.random.uniform(jax.random.fold_in(own, dim), (parts,), jnp.float32, smallest / len(cuts), high / len(cuts)))
        factor_of = factor_of * jnp.repeat(heights, dims[dim] // parts).reshape([-1 if axis == dim else 1 for axis in range(len(dims))])
    return factor_of


def gaussian(rng, extent, scale, limit, cuts=(), held_as=jnp.bfloat16):
    values = scale * jax.random.normal(rng, extent, jnp.float32)
    if cuts:
        values = values * levels(rng, extent, cuts, -0.22, 0.18)
    return jnp.clip(values, -limit, limit).astype(held_as)


def setup_inputs(seed: int = 0) -> dict:
    keys = jax.random.split(jax.random.key(seed), 6)
    video = draw_video(jax.random.fold_in(keys[5], 71), 0)
    conv_first = gaussian(keys[1], (27 * C, C), (27 * C) ** -0.5, 0.15625)
    conv_second = gaussian(keys[2], (27 * C, C), (27 * C) ** -0.5, 0.15625)
    conv_down = gaussian(keys[3], (27 * C, C_OUT), (27 * C) ** -0.5, 0.15625)
    down_cotangent = gaussian(keys[4], (CLIPS, FRAMES, ROWS // 2, (COLS // 2) * C_OUT), 1.0, 6.0, ((0, 2), (1, 32), (2, 2)))
    return {"video": video, "conv_first": conv_first, "conv_second": conv_second, "conv_down": conv_down, "down_cotangent": down_cotangent}


EPSILON = 1e-06

def swish(values):
    return values * jax.nn.sigmoid(values)

def round_half(values):
    return lax.optimization_barrier(values.astype(jnp.bfloat16)).astype(jnp.float32)

def conv_same(field, weight):
    kernel = weight.reshape(3, 3, 3, field.shape[-1], -1)
    result = lax.conv_general_dilated(field[None], kernel, (1, 1, 1), [(2, 0), (1, 1), (1, 1)], dimension_numbers=('NDHWC', 'DHWIO', 'NDHWC'), precision=lax.Precision.HIGHEST)
    return result[0]

def conv_half(field, weight):
    kernel = weight.reshape(3, 3, 3, field.shape[-1], -1)
    result = lax.conv_general_dilated(field[None], kernel, (1, 2, 2), [(2, 0), (1, 0), (1, 0)], dimension_numbers=('NDHWC', 'DHWIO', 'NDHWC'), precision=lax.Precision.HIGHEST)
    return result[0]

def group_view(values):
    return values.reshape(-1, GROUPS, values.shape[-1] // GROUPS)

def moments(values):
    grouped = group_view(values)
    centre = lax.optimization_barrier(jnp.mean(grouped, axis=(0, 2)))
    deviation = grouped - centre[None, :, None]
    variance = lax.optimization_barrier(jnp.mean(deviation * deviation, axis=(0, 2)))
    width = values.shape[-1] // GROUPS
    return (jnp.repeat(centre, width), jnp.repeat(lax.rsqrt(variance + EPSILON), width))

def norm_backward(grad_act, normed, inv_scale):
    sigma = jax.nn.sigmoid(normed)
    grad_normed = grad_act * sigma * (1.0 + normed * (1.0 - sigma))
    width = normed.shape[-1] // GROUPS
    first_mean = jnp.repeat(lax.optimization_barrier(jnp.mean(group_view(grad_normed), axis=(0, 2))), width)
    second_mean = jnp.repeat(lax.optimization_barrier(jnp.mean(group_view(grad_normed * normed), axis=(0, 2))), width)
    return inv_scale * (grad_normed - first_mean - normed * second_mean)

def reference(video, conv_first, conv_second, conv_down, down_cotangent):
    weight_one = conv_first.astype(jnp.float32)
    weight_two = conv_second.astype(jnp.float32)
    weight_down = conv_down.astype(jnp.float32)
    downs = []
    grads = []
    total_first = jnp.zeros(conv_first.shape, jnp.float32)
    total_second = jnp.zeros(conv_second.shape, jnp.float32)
    total_down = jnp.zeros(conv_down.shape, jnp.float32)
    for clip_index in range(N_CLIP):
        inputs = video[clip_index].reshape(FRAMES, ROWS, COLS, C).astype(jnp.float32)
        centre_one, scale_one = moments(inputs)
        normed_one = (inputs - centre_one) * scale_one
        act_one = round_half(swish(normed_one))
        hidden_one = round_half(conv_same(act_one, weight_one))
        centre_two, scale_two = moments(hidden_one)
        normed_two = (hidden_one - centre_two) * scale_two
        act_two = round_half(swish(normed_two))
        branch_out = conv_same(act_two, weight_two)
        block_out = round_half(inputs + branch_out)
        down_full, down_vjp = jax.vjp(conv_half, block_out, weight_down)
        downs.append(down_full.astype(jnp.bfloat16).reshape(FRAMES, ROWS // 2, COLS // 2 * C_OUT))
        cotangent = down_cotangent[clip_index].reshape(FRAMES, ROWS // 2, COLS // 2, C_OUT).astype(jnp.float32)
        grad_block, down_part = down_vjp(cotangent)
        second_out, second_vjp = jax.vjp(conv_same, act_two, weight_two)
        grad_act_two, second_part = second_vjp(round_half(grad_block))
        grad_hidden = round_half(norm_backward(grad_act_two, normed_two, scale_two))
        first_out, first_vjp = jax.vjp(conv_same, act_one, weight_one)
        grad_act_one, first_part = first_vjp(grad_hidden)
        grad_input = grad_block + norm_backward(grad_act_one, normed_one, scale_one)
        grads.append(grad_input.reshape(FRAMES, ROWS, COLS * C))
        total_first = total_first + first_part
        total_second = total_second + second_part
        total_down = total_down + down_part
    factor = 1.0 / math.sqrt(N_CLIP * FRAMES * ROWS * COLS)
    return (jnp.stack(downs), jnp.stack(grads), total_first * factor, total_second * factor, total_down * factor)
```

```python
import functools
import math

import jax
import jax.numpy as jnp
from jax import lax
from jax.experimental import pallas as pl
from jax.experimental.pallas import tpu as pltpu
from jax.sharding import PartitionSpec as P

MESH = pl.DeviceIdType.MESH
F32 = jnp.float32
BF16 = jnp.bfloat16
EPSILON = 1e-06
C = 64
C_OUT = 128
T = 4
R = 4
W = 80
L = 128
TM = 32
LOW = 8
HIGH = 8
WIDE = 16
PIECE_SD = 24
PIECE_F = 8
HALF = 864
CELLS = T * R * W
GROUP_CELLS = CELLS * 64


def low_peer(step):
    tm = lax.axis_index("tm")
    low = lax.rem(tm, LOW)
    return {"tm": tm - low + lax.rem(low + step, LOW)}


def high_peer(step):
    tm, space = lax.axis_index("tm"), lax.axis_index("space")
    place = lax.rem((tm // LOW) * 2 + space + step, HIGH)
    return {"tm": (place // 2) * LOW + lax.rem(tm, LOW), "space": lax.rem(place, 2)}


def wide_place():
    return ((lax.axis_index("tm") // LOW) * 2 + lax.axis_index("space")) * 2 + lax.axis_index("clip")


def wide_peer(step):
    tm = lax.axis_index("tm")
    place = lax.rem(wide_place() + step, WIDE)
    return {
        "tm": (place // 4) * LOW + lax.rem(tm, LOW),
        "space": lax.rem(place // 2, 2),
        "clip": lax.rem(place, 2),
    }


def near(step, across):
    tm, space = lax.axis_index("tm"), lax.axis_index("space")
    device = {}
    if step:
        device["tm"] = lax.rem(tm + step + TM, TM)
    if across:
        device["space"] = 1 - space
    return device


def ends(copies):
    for copy in copies:
        copy.wait()


def begins(copies):
    for copy in copies:
        copy.start()
    return copies


def lanes(shape):
    return lax.broadcasted_iota(jnp.int32, shape, len(shape) - 1)


def over_group(value):
    wide = jnp.broadcast_to(value, (8, L))
    both = wide + pltpu.roll(wide, C, 1)
    even = lax.rem(lanes((8, L)), 2) == 0
    other = jnp.where(even, pltpu.roll(both, L - 1, 1), pltpu.roll(both, 1, 1))
    return (both + other)[0:1]


def put_windows(target, f, r, x):
    turned = pltpu.roll(x, C, 1)
    row = lax.broadcasted_iota(jnp.int32, (W, L), 0)
    left = lanes((W, L)) < C
    above = jnp.where(row == 0, 0.0, pltpu.roll(turned, 1, 0))
    below = jnp.where(row == W - 1, 0.0, pltpu.roll(turned, W - 1, 0))
    target[f, r * W : (r + 1) * W, 0:L] = jnp.where(left, above, turned).astype(BF16)
    target[f, r * W : (r + 1) * W, L : 2 * L] = jnp.where(left, turned, below).astype(BF16)


def conv(windows, weights, t):
    total = None
    for dt in range(3):
        for dr in range(3):
            part = jnp.dot(
                windows[t + dt, dr * W : (dr + R) * W, :],
                weights[dt * 3 + dr],
                preferred_element_type=F32,
            )
            total = part if total is None else total + part
    return total


def transposed(source):
    return source.T.astype(BF16)


def kernel(
    video, cot, w_first, w_second, b_first, b_second, w_down, b_down,
    out_down, out_video, out_first, out_second, out_grad_down,
    v_ext, field, c_ext, c_field, c_win, g_block, g_ext, h_ext, t2_ext, t1, win_first, win_second,
    win_back, b_ext, b_even, b_odd, gt, gtc, st_src, st_buf,
    full_sd, send_sd, recv_sd, sum_sd, recvb_sd, total_sd, gather_sd, all_sd,
    full_f, send_f, recv_f, sum_f, recvb_f, total_f, gather_f, all_f,
    halo_sems, st_sems, wa_sems, wb_sems, wc_sems, wd_sems,
):
    tm, space = lax.axis_index("tm"), lax.axis_index("space")
    low = lax.rem(tm, LOW)
    high = (tm // LOW) * 2 + space
    place = wide_place()
    has_past = jnp.where(tm == 0, 0.0, 1.0).astype(F32)
    has_next = jnp.where(tm == TM - 1, 0.0, 1.0).astype(F32)
    has_above = jnp.where(space == 0, 0.0, 1.0).astype(F32)
    has_below = jnp.where(space == 1, 0.0, 1.0).astype(F32)
    one = jnp.ones((), F32)

    def row_mask(r):
        return has_above if r == 0 else has_below if r == R + 1 else one

    edge = pl.multiple_of((R - (R - 1) * space) * W, W)
    far = pl.multiple_of((R + 1) * space * W, W)

    peers = [low_peer(k) for k in range(1, LOW)] + [wide_peer(k) for k in range(1, WIDE)]
    peers += [near(1, False), near(-1, False), near(1, True), near(-1, True)]
    barrier = pltpu.get_barrier_semaphore()
    for peer in peers:
        pl.semaphore_signal(barrier, inc=1, device_id=peer, device_id_type=MESH)

    def remote(source, target, send, recv, device):
        return pltpu.make_async_remote_copy(
            src_ref=source, dst_ref=target, send_sem=send, recv_sem=recv,
            device_id=device, device_id_type=MESH,
        )

    def halo(slot, source, target, device):
        return remote(source, target, halo_sems.at[0, slot], halo_sems.at[1, slot], device)

    def send_stats(k, stage):
        me, peer, size = (low, low_peer, LOW) if stage == 0 else (high, high_peer, HIGH)
        copies = begins([
            remote(
                st_src.at[k, stage], st_buf.at[k, stage, me],
                st_sems.at[0, k, stage, j], st_sems.at[1, k, stage, j], peer(j),
            )
            for j in range(1, size)
        ])
        st_buf[k, stage, me] = st_src[k, stage]
        return copies

    def join_stats(k, stage, copies, centred):
        ends(copies)
        parts = [st_buf[k, stage, j] for j in range(LOW)]
        total = parts[0]
        for part in parts[1:]:
            total = total + part
        first, second = total[0:1], total[1:2]
        if centred:
            cells = float(CELLS * (1 if stage == 0 else LOW))
            first = first * (1.0 / LOW)
            for part in parts:
                second = second + cells * ((part[0:1] - first) * (part[0:1] - first))
        return first, second

    def put_stats(k, stage, first, second):
        st_src[k, stage] = jnp.zeros((8, L), F32)
        st_src[k, stage, 0:1] = first
        st_src[k, stage, 1:2] = second

    def scale_of(mean, spread):
        centre = over_group(mean) * 0.25
        gap = mean - centre
        variance = over_group(spread + float(GROUP_CELLS) * (gap * gap)) * (1.0 / (4 * GROUP_CELLS))
        return centre, lax.rsqrt(variance + EPSILON)

    def spread_of(mean, read):
        def step(t, total):
            gap = read(t) - mean
            return total + jnp.sum(gap * gap, axis=0, keepdims=True)

        return lax.fori_loop(0, T, step, jnp.zeros((1, L), F32))

    def take_video(t, total):
        for p in range(W):
            field[t, pl.ds(p, R, stride=W), :] = video[0, t, :, p * L : (p + 1) * L].astype(F32)
        value = field[t]
        v_ext[t + 2, W : (R + 1) * W, :] = value.astype(BF16)
        return total + jnp.sum(value, axis=0, keepdims=True)

    mean = lax.fori_loop(0, T, take_video, jnp.zeros((1, L), F32)) * (1.0 / CELLS)
    put_stats(0, 0, mean, spread_of(mean, lambda t: field[t]))
    pl.semaphore_wait(barrier, len(peers))
    stats = send_stats(0, 0)
    own = pl.ds(W, R * W)
    video_halo = begins([
        halo(0, v_ext.at[T : T + 2, own], v_ext.at[0:2, own], near(1, False)),
        halo(1, v_ext.at[2 : T + 2, pl.ds(edge, W)], v_ext.at[2 : T + 2, pl.ds(far, W)], near(0, True)),
        halo(2, v_ext.at[T : T + 2, pl.ds(edge, W)], v_ext.at[0:2, pl.ds(far, W)], near(1, True)),
    ])
    for ref in (v_ext, g_ext, h_ext, t2_ext):
        for f in range(ref.shape[0]):
            ref[f, pl.ds(far, W), :] = jnp.zeros((W, L), ref.dtype)

    @pl.loop(0, T)
    def _(t):
        for p in range(W):
            c_field[t, pl.ds(p, 2, stride=W), :] = cot[0, t, :, p * L : (p + 1) * L].astype(F32)
        c_ext[t, 0 : 2 * W, :] = c_field[t].astype(BF16)

    cot_halo = begins([
        halo(3, c_ext.at[0:2, pl.ds(0, 2 * W)], c_ext.at[T : T + 2, pl.ds(0, 2 * W)], near(-1, False)),
        halo(4, c_ext.at[0:T, pl.ds(0, W)], c_ext.at[0:T, pl.ds(2 * W, W)], near(0, True)),
        halo(5, c_ext.at[0:2, pl.ds(0, W)], c_ext.at[T : T + 2, pl.ds(2 * W, W)], near(-1, True)),
    ])
    for half in range(2):
        both = c_field[2 * half : 2 * half + 2].reshape(4 * W, L)
        gtc[:, half * 4 * W : half * 4 * W + 4 * W] = transposed(both)
    put_stats(0, 1, *join_stats(0, 0, stats, True))
    stats = send_stats(0, 1)
    ends(cot_halo)

    @pl.loop(0, T + 2)
    def _(f):
        late = jnp.where(f >= T, has_next, one)
        for r in range(3):
            value = c_ext[f, r * W : (r + 1) * W, :].astype(F32) * (late * has_below if r == 2 else late)
            row = lax.broadcasted_iota(jnp.int32, (W, L), 0)
            after = jnp.where(row == W - 1, 0.0, pltpu.roll(value, W - 1, 0))
            c_win[f, r * W : (r + 1) * W, 0:L] = value.astype(BF16)
            c_win[f, r * W : (r + 1) * W, L : 2 * L] = after.astype(BF16)

    @pl.loop(0, T)
    def _(t):
        even = odd = None
        for j in range(3):
            here = c_win[t + j, 0 : 2 * W, :]
            below = c_win[t + j, W : 3 * W, :]
            a = jnp.dot(here, b_down[j * 3 + 1], preferred_element_type=F32)
            b = jnp.dot(here, b_down[j * 3], preferred_element_type=F32)
            b = b + jnp.dot(below, b_down[j * 3 + 2], preferred_element_type=F32)
            even, odd = (a, b) if j == 0 else (even + a, odd + b)
        for i in range(2):
            for parity, value in ((0, even), (1, odd)):
                r = 2 * i + parity
                piece = value[i * W : (i + 1) * W]
                g_block[t, r * W : (r + 1) * W, :] = piece
                g_ext[t, (r + 1) * W : (r + 2) * W, :] = piece.astype(BF16)

    grad_halo = begins([
        halo(6, g_ext.at[0:2, own], g_ext.at[T : T + 2, own], near(-1, False)),
        halo(7, g_ext.at[0:T, pl.ds(edge, W)], g_ext.at[0:T, pl.ds(far, W)], near(0, True)),
        halo(8, g_ext.at[0:2, pl.ds(edge, W)], g_ext.at[T : T + 2, pl.ds(far, W)], near(-1, True)),
    ])
    for half in range(2):
        both = g_ext[2 * half : 2 * half + 2, W : (R + 1) * W, :].reshape(8 * W, L)
        gt[:, half * 8 * W : (half + 1) * 8 * W] = transposed(both.astype(F32))

    centre_one, scale_one = scale_of(*join_stats(0, 1, stats, True))
    ends(video_halo)

    @pl.loop(0, T + 2)
    def _(f):
        early = jnp.where(f < 2, has_past, one)
        for r in range(R + 2):
            normed = (v_ext[f, r * W : (r + 1) * W, :].astype(F32) - centre_one) * scale_one
            put_windows(win_first, f, r, normed * jax.nn.sigmoid(normed) * (early * row_mask(r)))

    def first_conv(t, total):
        hidden = conv(win_first, w_first, t).astype(BF16)
        h_ext[t + 2, W : (R + 1) * W, :] = hidden
        return total + jnp.sum(hidden.astype(F32), axis=0, keepdims=True)

    mean = lax.fori_loop(0, T, first_conv, jnp.zeros((1, L), F32)) * (1.0 / CELLS)

    def own_hidden(t):
        return h_ext[t + 2, W : (R + 1) * W, :].astype(F32)

    put_stats(1, 0, mean, spread_of(mean, own_hidden))
    stats = send_stats(1, 0)
    hidden_halo = begins([
        halo(9, h_ext.at[T : T + 2, own], h_ext.at[0:2, own], near(1, False)),
        halo(10, h_ext.at[2 : T + 2, pl.ds(edge, W)], h_ext.at[2 : T + 2, pl.ds(far, W)], near(0, True)),
        halo(11, h_ext.at[T : T + 2, pl.ds(edge, W)], h_ext.at[0:2, pl.ds(far, W)], near(1, True)),
        halo(12, h_ext.at[2:4, own], h_ext.at[T + 2 : T + 4, own], near(-1, False)),
        halo(13, h_ext.at[2:4, pl.ds(edge, W)], h_ext.at[T + 2 : T + 4, pl.ds(far, W)], near(-1, True)),
    ])

    ends(grad_halo)

    @pl.loop(0, T + 2)
    def _(f):
        late = jnp.where(f >= T, has_next, one)
        for r in range(R + 2):
            value = g_ext[f, r * W : (r + 1) * W, :].astype(F32) * (late * row_mask(r))
            put_windows(win_back, f, r, value)

    put_stats(1, 1, *join_stats(1, 0, stats, True))
    stats = send_stats(1, 1)

    @pl.loop(0, T)
    def _(t):
        t2_ext[t, W : (R + 1) * W, :] = conv(win_back, b_second, t)

    act_halo = begins([
        halo(14, t2_ext.at[0:2, own], t2_ext.at[T : T + 2, own], near(-1, False)),
        halo(15, t2_ext.at[0:T, pl.ds(edge, W)], t2_ext.at[0:T, pl.ds(far, W)], near(0, True)),
        halo(16, t2_ext.at[0:2, pl.ds(edge, W)], t2_ext.at[T : T + 2, pl.ds(far, W)], near(-1, True)),
    ])

    centre_two, scale_two = scale_of(*join_stats(1, 1, stats, True))

    def gradient(grad, normed):
        sigma = jax.nn.sigmoid(normed)
        return grad * sigma * (1.0 + normed * (1.0 - sigma))

    def second_sums(t, sums):
        first, second = sums
        for r in range(1, R + 1):
            normed = (h_ext[t + 2, r * W : (r + 1) * W, :].astype(F32) - centre_two) * scale_two
            grad = gradient(t2_ext[t, r * W : (r + 1) * W, :], normed)
            first = first + jnp.sum(grad, axis=0, keepdims=True)
            second = second + jnp.sum(grad * normed, axis=0, keepdims=True)
        return first, second

    nothing = (jnp.zeros((1, L), F32), jnp.zeros((1, L), F32))
    put_stats(2, 0, *lax.fori_loop(0, T, second_sums, nothing))
    stats = send_stats(2, 0)
    ends(hidden_halo)

    @pl.loop(0, T + 2)
    def _(f):
        early = jnp.where(f < 2, has_past, one)
        for r in range(R + 2):
            normed = (h_ext[f, r * W : (r + 1) * W, :].astype(F32) - centre_two) * scale_two
            put_windows(win_second, f, r, normed * jax.nn.sigmoid(normed) * (early * row_mask(r)))

    put_stats(2, 1, *join_stats(2, 0, stats, False))
    stats = send_stats(2, 1)

    @pl.loop(0, T)
    def _(t):
        block = v_ext[t + 2, W : (R + 1) * W, :].astype(F32) + conv(win_second, w_second, t)
        b_ext[t + 2, W : (R + 1) * W, :] = block.astype(BF16)

    block_halo = begins([
        halo(17, b_ext.at[T : T + 2, own], b_ext.at[0:2, own], near(1, False)),
        halo(18, b_ext.at[2 : T + 2, pl.ds(R * W, W)], b_ext.at[2 : T + 2, pl.ds(0, W)], near(0, True)),
        halo(19, b_ext.at[T : T + 2, pl.ds(R * W, W)], b_ext.at[0:2, pl.ds(0, W)], near(1, True)),
    ])

    def block_weights(windows, full, base):
        left = lanes((3 * C, L)) < C

        def folded(dt, dr):
            cells = windows[dt : dt + T, dr * W : (dr + R) * W, :].reshape(CELLS, 2 * L)
            turned = jnp.dot(gt[...], cells, preferred_element_type=F32).T
            return turned[0 : 3 * C] + pltpu.roll(turned[C : 4 * C], C, 1)

        for pair in range(4):
            a, b = 2 * pair, 2 * pair + 1
            value = jnp.where(left, folded(a // 3, a % 3), pltpu.roll(folded(b // 3, b % 3), C, 1))
            full[base + pair * 3 * C : base + (pair + 1) * 3 * C, :] = value
        value = folded(2, 2)
        half = 3 * C // 2
        value = jnp.where(left[0:half], value[0:half], pltpu.roll(value[half:], C, 1))
        full[base + 12 * C : base + 12 * C + half, :] = value

    full_sd[HALF + 27 * C :, :] = jnp.zeros((full_sd.shape[0] - HALF - 27 * C, L), F32)
    full_f[HALF:, :] = jnp.zeros((full_f.shape[0] - HALF, L), F32)
    block_weights(win_second, full_sd, 0)

    ends(block_halo)

    @pl.loop(0, T + 2)
    def _(f):
        early = jnp.where(f < 2, has_past, one)
        for r in range(R + 1):
            value = b_ext[f, r * W : (r + 1) * W, :].astype(F32) * (early * has_above if r == 0 else early)
            put_windows(b_odd if r % 2 else b_even, f, r // 2, value)

    def projected(dr):
        return (b_even, 0) if dr == 0 else (b_odd, 0) if dr == 1 else (b_even, W)

    @pl.loop(0, T)
    def _(t):
        total = None
        for dt in range(3):
            for dr in range(3):
                ref, start = projected(dr)
                part = jnp.dot(
                    ref[t + dt, start : start + 2 * W, 0 : 3 * C],
                    w_down[dt * 3 + dr],
                    preferred_element_type=F32,
                )
                total = part if total is None else total + part
        c_field[t] = total
        for p in range(W):
            out_down[0, t, :, p * L : (p + 1) * L] = c_field[t, pl.ds(p, 2, stride=W), :].astype(BF16)

    for dt in range(3):
        for dr in range(3):
            ref, start = projected(dr)
            cells = ref[dt : dt + T, start : start + 2 * W, :].reshape(2 * W * T, 2 * L)
            turned = jnp.dot(gtc[...], cells, preferred_element_type=F32).T
            base = HALF + (dt * 3 + dr) * 3 * C
            full_sd[base : base + 3 * C, :] = turned[0 : 3 * C]

    def part_of(index, rows):
        return pl.ds(pl.multiple_of(index * rows, 8), rows)

    class Reduction:
        def __init__(self, number, piece, full, send, recv, sums, recvb, total, gather, whole):
            self.n, self.piece, self.rows = number, piece, piece * WIDE
            self.full, self.send, self.recv, self.sums = full, send, recv, sums
            self.recvb, self.total, self.gather, self.whole = recvb, total, gather, whole

        def sem(self, sems, k):
            return sems.at[0, self.n, k], sems.at[1, self.n, k]

        def start(self):
            self.send[...] = self.full[...].astype(BF16)
            self.copies = begins([
                remote(
                    self.send.at[part_of(lax.rem(low + k, LOW), self.rows)], self.recv.at[k - 1],
                    *self.sem(wa_sems, k), low_peer(k),
                )
                for k in range(1, LOW)
            ])

        def second(self):
            ends(self.copies)
            value = self.full[part_of(low, self.rows), :]
            for k in range(LOW - 1):
                value = value + self.recv[k].astype(F32)
            self.sums[...] = value
            self.copies = begins([
                remote(
                    self.sums.at[part_of(lax.rem(place + k, WIDE), self.piece)], self.recvb.at[k - 1],
                    *self.sem(wb_sems, k), wide_peer(k),
                )
                for k in range(1, WIDE)
            ])

        def third(self):
            ends(self.copies)
            value = self.sums[part_of(place, self.piece), :]
            for k in range(WIDE - 1):
                value = value + self.recvb[k]
            value = value * (1.0 / math.sqrt(2 * 128 * 8 * 160))
            self.total[...] = value
            self.copies = begins([
                remote(
                    self.total, self.gather.at[part_of(place, self.piece)],
                    *self.sem(wc_sems, k), wide_peer(k),
                )
                for k in range(1, WIDE)
            ])
            self.gather[part_of(place, self.piece), :] = value

        def fourth(self):
            ends(self.copies)
            here = pl.ds(pl.multiple_of(low * self.rows, 16), self.rows)
            self.whole[here, :] = self.gather[...].astype(BF16)
            self.copies = begins([
                remote(
                    self.whole.at[here], self.whole.at[here], *self.sem(wd_sems, k), low_peer(k),
                )
                for k in range(1, LOW)
            ])

        def finish(self):
            ends(self.copies)

    sums_sd = Reduction(0, PIECE_SD, full_sd, send_sd, recv_sd, sum_sd, recvb_sd, total_sd, gather_sd, all_sd)
    sums_f = Reduction(1, PIECE_F, full_f, send_f, recv_f, sum_f, recvb_f, total_f, gather_f, all_f)
    sums_sd.start()

    count = 1.0 / (4 * GROUP_CELLS)
    ends(act_halo)
    first, second = join_stats(2, 1, stats, False)
    mean_one, mean_two = over_group(first) * count, over_group(second) * count

    @pl.loop(0, T + 2)
    def _(f):
        late = jnp.where(f >= T, has_next, one)
        for r in range(R + 2):
            normed = (h_ext[f + 2, r * W : (r + 1) * W, :].astype(F32) - centre_two) * scale_two
            grad = gradient(t2_ext[f, r * W : (r + 1) * W, :], normed)
            hidden = scale_two * (grad - mean_one - normed * mean_two)
            put_windows(win_back, f, r, hidden * (late * row_mask(r)))
            if 1 <= r <= R:

                @pl.when(f < T)
                def _():
                    field[f, (r - 1) * W : r * W, :] = hidden

    def back_first(t, sums):
        back = conv(win_back, b_first, t)
        normed = (v_ext[t + 2, W : (R + 1) * W, :].astype(F32) - centre_one) * scale_one
        grad = gradient(back, normed)
        t1[t] = grad
        return (
            sums[0] + jnp.sum(grad, axis=0, keepdims=True),
            sums[1] + jnp.sum(grad * normed, axis=0, keepdims=True),
        )

    put_stats(3, 0, *lax.fori_loop(0, T, back_first, nothing))
    stats = send_stats(3, 0)
    sums_sd.second()
    for half in range(2):
        both = field[2 * half : 2 * half + 2].reshape(8 * W, L)
        gt[:, half * 8 * W : (half + 1) * 8 * W] = transposed(both)
    block_weights(win_first, full_f, 0)
    sums_f.start()
    put_stats(3, 1, *join_stats(3, 0, stats, False))
    stats = send_stats(3, 1)
    sums_sd.third()
    sums_f.second()
    first, second = join_stats(3, 1, stats, False)
    mean_one, mean_two = over_group(first) * count, over_group(second) * count
    sums_sd.fourth()

    @pl.loop(0, T)
    def _(t):
        normed = (v_ext[t + 2, W : (R + 1) * W, :].astype(F32) - centre_one) * scale_one
        field[t] = g_block[t] + scale_one * (t1[t] - mean_one - normed * mean_two)
        for p in range(W):
            out_video[0, t, :, p * L : (p + 1) * L] = field[t, pl.ds(p, R, stride=W), :]

    sums_f.third()
    sums_f.fourth()

    def unpack(source, base, target):
        for pair in range(4):
            value = source[base + pair * 3 * C : base + (pair + 1) * 3 * C, :].astype(F32)
            target[pair * 6 * C : pair * 6 * C + 3 * C, :] = value[:, 0:C]
            target[pair * 6 * C + 3 * C : (pair + 1) * 6 * C, :] = pltpu.roll(value, C, 1)[:, 0:C]
        half = 3 * C // 2
        value = source[base + 12 * C : base + 12 * C + half, :].astype(F32)
        target[24 * C : 24 * C + half, :] = value[:, 0:C]
        target[24 * C + half : 27 * C, :] = pltpu.roll(value, C, 1)[:, 0:C]

    sums_sd.finish()
    unpack(all_sd, 0, out_second)
    out_grad_down[...] = all_sd[HALF : HALF + 27 * C, :].astype(F32)
    sums_f.finish()
    unpack(all_f, 0, out_first)


def windowed(kernels):
    flat = kernels.reshape(9, 3 * C, C)
    empty = jnp.zeros((9, C, C), flat.dtype)
    return jnp.concatenate(
        [jnp.concatenate([flat, empty], axis=1), jnp.concatenate([empty, flat], axis=1)], axis=2
    )


def flipped(weight, channels):
    return jnp.swapaxes(weight.reshape(27, C, channels)[::-1], 1, 2)


def local(video, conv_first, conv_second, conv_down, down_cotangent):
    back_down = flipped(conv_down, C_OUT).reshape(9, 3, C_OUT, C)
    upper = jnp.concatenate([back_down[:, 1], back_down[:, 0]], axis=2)
    lower = jnp.concatenate([jnp.zeros_like(back_down[:, 2]), back_down[:, 2]], axis=2)
    operands = (
        video,
        down_cotangent,
        windowed(conv_first.reshape(9, 3, C, C)),
        windowed(conv_second.reshape(9, 3, C, C)),
        windowed(flipped(conv_first, C).reshape(9, 3, C, C)),
        windowed(flipped(conv_second, C).reshape(9, 3, C, C)),
        conv_down.reshape(9, 3 * C, C_OUT),
        jnp.concatenate([upper, lower], axis=1),
    )
    rows = (R + 2) * W

    def reduction(piece):
        total, part = piece * WIDE * LOW, piece * WIDE
        return [
            pltpu.VMEM((total, L), F32),
            pltpu.VMEM((total, L), BF16),
            pltpu.VMEM((LOW - 1, part, L), BF16),
            pltpu.VMEM((part, L), F32),
            pltpu.VMEM((WIDE - 1, piece, L), F32),
            pltpu.VMEM((piece, L), F32),
            pltpu.VMEM((part, L), F32),
            pltpu.VMEM((total, L), BF16),
        ]

    vmem = pl.BlockSpec(memory_space=pltpu.VMEM)
    dma = pltpu.SemaphoreType.DMA
    return pl.pallas_call(
        kernel,
        out_shape=(
            jax.ShapeDtypeStruct((1, T, 2, W * L), BF16),
            jax.ShapeDtypeStruct((1, T, R, W * L), F32),
            jax.ShapeDtypeStruct((27 * C, C), F32),
            jax.ShapeDtypeStruct((27 * C, C), F32),
            jax.ShapeDtypeStruct((27 * C, C_OUT), F32),
        ),
        in_specs=[vmem] * len(operands),
        out_specs=(vmem,) * 5,
        scratch_shapes=[
            pltpu.VMEM((T + 2, rows, L), BF16),
            pltpu.VMEM((T, R * W, L), F32),
            pltpu.VMEM((T + 2, 3 * W, L), BF16),
            pltpu.VMEM((T, 2 * W, L), F32),
            pltpu.VMEM((T + 2, 3 * W, 2 * L), BF16),
            pltpu.VMEM((T, R * W, L), F32),
            pltpu.VMEM((T + 2, rows, L), BF16),
            pltpu.VMEM((T + 4, rows, L), BF16),
            pltpu.VMEM((T + 2, rows, L), F32),
            pltpu.VMEM((T, R * W, L), F32),
            pltpu.VMEM((T + 2, rows, 2 * L), BF16),
            pltpu.VMEM((T + 2, rows, 2 * L), BF16),
            pltpu.VMEM((T + 2, rows, 2 * L), BF16),
            pltpu.VMEM((T + 2, (R + 1) * W, L), BF16),
            pltpu.VMEM((T + 2, 3 * W, 2 * L), BF16),
            pltpu.VMEM((T + 2, 2 * W, 2 * L), BF16),
            pltpu.VMEM((L, CELLS), BF16),
            pltpu.VMEM((L, CELLS // 2), BF16),
            pltpu.VMEM((4, 2, 8, L), F32),
            pltpu.VMEM((4, 2, LOW, 8, L), F32),
            *reduction(PIECE_SD),
            *reduction(PIECE_F),
            dma((2, 20)),
            dma((2, 4, 2, LOW)),
            dma((2, 2, LOW)),
            dma((2, 2, WIDE)),
            dma((2, 2, WIDE)),
            dma((2, 2, LOW)),
        ],
        compiler_params=pltpu.CompilerParams(
            collective_id=1, has_side_effects=True, vmem_limit_bytes=56 * 1024 * 1024
        ),
    )(*operands)


def solution(mesh):
    in_specs = (P("clip", "tm", "space", None), P(), P(), P(), P("clip", "tm", "space", None))
    out_specs = (P("clip", "tm", "space", None), P("clip", "tm", "space", None), P(), P(), P())
    return jax.shard_map(local, mesh=mesh, in_specs=in_specs, out_specs=out_specs, check_vma=False)
```

```python
import functools
import math

import jax
import jax.numpy as jnp
from jax import lax
from jax.experimental import pallas as pl
from jax.experimental.pallas import tpu as pltpu
from jax.sharding import PartitionSpec as P

MESH = pl.DeviceIdType.MESH
F32 = jnp.float32
BF16 = jnp.bfloat16
EPSILON = 1e-06
C = 64
C_OUT = 128
T = 4
R = 4
W = 80
L = 128
TM = 32
LOW = 8
HIGH = 8
PLANE = 16
COLUMN = 8
PIECE_SD = 176
PIECE_F = 64
TILES = 14
HALF = TILES * C
CELLS = T * R * W
GROUP_CELLS = CELLS * 64


def low_peer(step):
    tm = lax.axis_index("tm")
    low = lax.rem(tm, LOW)
    return {"tm": tm - low + lax.rem(low + step, LOW)}


def high_peer(step):
    tm, space = lax.axis_index("tm"), lax.axis_index("space")
    place = lax.rem((tm // LOW) * 2 + space + step, HIGH)
    return {"tm": (place // 2) * LOW + lax.rem(tm, LOW), "space": lax.rem(place, 2)}


def plane_place():
    return lax.axis_index("tm") // 2


def plane_peer(step):
    tm = lax.axis_index("tm")
    return {"tm": lax.rem(tm // 2 + step, PLANE) * 2 + lax.rem(tm, 2)}


def column_place():
    core = lax.rem(lax.axis_index("tm"), 2)
    return (core * 2 + lax.axis_index("space")) * 2 + lax.axis_index("clip")


def column_peer(step):
    tm = lax.axis_index("tm")
    place = lax.rem(column_place() + step, COLUMN)
    return {
        "tm": (tm // 2) * 2 + place // 4,
        "space": lax.rem(place // 2, 2),
        "clip": lax.rem(place, 2),
    }


def near(step, across):
    tm, space = lax.axis_index("tm"), lax.axis_index("space")
    device = {}
    if step:
        device["tm"] = lax.rem(tm + step + TM, TM)
    if across:
        device["space"] = 1 - space
    return device


def ends(copies):
    for copy in copies:
        copy.wait()


def begins(copies):
    for copy in copies:
        copy.start()
    return copies


def lanes(shape):
    return lax.broadcasted_iota(jnp.int32, shape, len(shape) - 1)


def over_group(value):
    wide = jnp.broadcast_to(value, (8, L))
    both = wide + pltpu.roll(wide, C, 1)
    even = lax.rem(lanes((8, L)), 2) == 0
    other = jnp.where(even, pltpu.roll(both, L - 1, 1), pltpu.roll(both, 1, 1))
    return (both + other)[0:1]


def put_windows(target, f, r, x):
    turned = pltpu.roll(x, C, 1)
    row = lax.broadcasted_iota(jnp.int32, (W, L), 0)
    left = lanes((W, L)) < C
    above = jnp.where(row == 0, 0.0, pltpu.roll(turned, 1, 0))
    below = jnp.where(row == W - 1, 0.0, pltpu.roll(turned, W - 1, 0))
    target[f, r * W : (r + 1) * W, 0:L] = jnp.where(left, above, turned).astype(BF16)
    target[f, r * W : (r + 1) * W, L : 2 * L] = jnp.where(left, turned, below).astype(BF16)


def dot_turned(a, b):
    return lax.dot_general(a, b, (((1,), (1,)), ((), ())), preferred_element_type=F32)


def dot(a, b):
    return jnp.dot(a, b, preferred_element_type=F32)


def conv(windows, weights, t, multiply):
    total = None
    for dt in range(3):
        for dr in range(3):
            part = multiply(windows[t + dt, dr * W : (dr + R) * W, :], weights[dt * 3 + dr])
            total = part if total is None else total + part
    return total


def put_kernels(raw, padded, ahead, back):
    width = 27 * C
    padded[:, 0:width] = raw[...].astype(F32)
    padded[:, width:] = jnp.zeros((C, padded.shape[1] - width), F32)
    lane = lanes((C, 4 * C))
    for tap in range(9):
        start = tap * 3 * C
        if tap % 2 == 0:
            near = jnp.where(lane < 3 * C, padded[:, start : start + 4 * C], 0.0)
            later = pltpu.roll(near, C, 1)
        else:
            later = jnp.where(lane < C, 0.0, padded[:, start - C : start + 3 * C])
            near = pltpu.roll(later, 3 * C, 1)
        near, later = near.astype(BF16), later.astype(BF16)
        ahead[tap, 0:C, :] = near
        ahead[tap, C : 2 * C, :] = later
        back[8 - tap, 0:C, :] = near[:, 2 * C :]
        back[8 - tap, C : 2 * C, :] = later[:, 2 * C :]
        back[8 - tap, 2 * C : 3 * C, :] = near[:, 0 : 2 * C]
        back[8 - tap, 3 * C : 4 * C, :] = later[:, 0 : 2 * C]


def sigmoid(value):
    return 0.5 + 0.5 * jnp.tanh(0.5 * value)


def transposed(source):
    return source.T.astype(BF16)


def kernel(
    video, cot, raw_first, raw_second, w_down,
    out_down, out_video, all_sd, all_f,
    padded, w_first, w_second, b_first, b_second, b_down,
    v_ext, field, c_ext, c_field, c_win, g_block, g_ext, h_ext, t2_ext, t1, win_first, win_second,
    win_back, b_ext, b_even, b_odd, gt, gtc, st_src, st_buf,
    full_sd, send_sd, recv_sd, sum_sd, recvb_sd,
    full_f, send_f, recv_f, sum_f, recvb_f,
    halo_sems, st_sems, wa_sems, wb_sems, wc_sems,
):
    tm, space = lax.axis_index("tm"), lax.axis_index("space")
    low = lax.rem(tm, LOW)
    high = (tm // LOW) * 2 + space
    plane, column = plane_place(), column_place()
    has_past = jnp.where(tm == 0, 0.0, 1.0).astype(F32)
    has_next = jnp.where(tm == TM - 1, 0.0, 1.0).astype(F32)
    has_above = jnp.where(space == 0, 0.0, 1.0).astype(F32)
    has_below = jnp.where(space == 1, 0.0, 1.0).astype(F32)
    one = jnp.ones((), F32)

    def row_mask(r):
        return has_above if r == 0 else has_below if r == R + 1 else one

    edge = pl.multiple_of((R - (R - 1) * space) * W, W)
    far = pl.multiple_of((R + 1) * space * W, W)

    peers = [low_peer(k) for k in range(1, LOW)] + [high_peer(k) for k in range(1, HIGH)]
    peers += [plane_peer(k) for k in range(1, PLANE)] + [column_peer(k) for k in range(1, COLUMN)]
    peers += [near(1, False), near(-1, False), near(1, True), near(-1, True)]
    barrier = pltpu.get_barrier_semaphore()
    for peer in peers:
        pl.semaphore_signal(barrier, inc=1, device_id=peer, device_id_type=MESH)

    def remote(source, target, send, recv, device):
        return pltpu.make_async_remote_copy(
            src_ref=source, dst_ref=target, send_sem=send, recv_sem=recv,
            device_id=device, device_id_type=MESH,
        )

    def halo(slot, source, target, device):
        return remote(source, target, halo_sems.at[0, slot], halo_sems.at[1, slot], device)

    def send_stats(k, stage):
        me, peer, size = (low, low_peer, LOW) if stage == 0 else (high, high_peer, HIGH)
        copies = begins([
            remote(
                st_src.at[k, stage], st_buf.at[k, stage, me],
                st_sems.at[0, k, stage, j], st_sems.at[1, k, stage, j], peer(j),
            )
            for j in range(1, size)
        ])
        st_buf[k, stage, me] = st_src[k, stage]
        return copies

    def join_stats(k, stage, copies, centred):
        ends(copies)
        parts = [st_buf[k, stage, j] for j in range(LOW)]
        total = parts[0]
        for part in parts[1:]:
            total = total + part
        first, second = total[0:1], total[1:2]
        if centred:
            cells = float(CELLS * (1 if stage == 0 else LOW))
            first = first * (1.0 / LOW)
            for part in parts:
                second = second + cells * ((part[0:1] - first) * (part[0:1] - first))
        return first, second

    def put_stats(k, stage, first, second):
        st_src[k, stage] = jnp.zeros((8, L), F32)
        st_src[k, stage, 0:1] = first
        st_src[k, stage, 1:2] = second

    def scale_of(mean, spread):
        centre = over_group(mean) * 0.25
        gap = mean - centre
        variance = over_group(spread + float(GROUP_CELLS) * (gap * gap)) * (1.0 / (4 * GROUP_CELLS))
        return centre, lax.rsqrt(variance + EPSILON)

    def spread_of(mean, read):
        def step(t, total):
            gap = read(t) - mean
            return total + jnp.sum(gap * gap, axis=0, keepdims=True)

        return lax.fori_loop(0, T, step, jnp.zeros((1, L), F32))

    def take_video(t, total):
        for p in range(W):
            field[t, pl.ds(p, R, stride=W), :] = video[0, t, :, p * L : (p + 1) * L].astype(F32)
        value = field[t]
        v_ext[t + 2, W : (R + 1) * W, :] = value.astype(BF16)
        return total + jnp.sum(value, axis=0, keepdims=True)

    mean = lax.fori_loop(0, T, take_video, jnp.zeros((1, L), F32)) * (1.0 / CELLS)
    put_stats(0, 0, mean, spread_of(mean, lambda t: field[t]))
    pl.semaphore_wait(barrier, len(peers))
    stats = send_stats(0, 0)
    own = pl.ds(W, R * W)
    video_halo = begins([
        halo(0, v_ext.at[T : T + 2, own], v_ext.at[0:2, own], near(1, False)),
        halo(1, v_ext.at[2 : T + 2, pl.ds(edge, W)], v_ext.at[2 : T + 2, pl.ds(far, W)], near(0, True)),
        halo(2, v_ext.at[T : T + 2, pl.ds(edge, W)], v_ext.at[0:2, pl.ds(far, W)], near(1, True)),
    ])
    for ref in (v_ext, g_ext, h_ext, t2_ext):
        for f in range(ref.shape[0]):
            ref[f, pl.ds(far, W), :] = jnp.zeros((W, L), ref.dtype)

    @pl.loop(0, T)
    def _(t):
        for p in range(W):
            c_field[t, pl.ds(p, 2, stride=W), :] = cot[0, t, :, p * L : (p + 1) * L].astype(F32)
        c_ext[t, 0 : 2 * W, :] = c_field[t].astype(BF16)

    cot_halo = begins([
        halo(3, c_ext.at[0:2, pl.ds(0, 2 * W)], c_ext.at[T : T + 2, pl.ds(0, 2 * W)], near(-1, False)),
        halo(4, c_ext.at[0:T, pl.ds(0, W)], c_ext.at[0:T, pl.ds(2 * W, W)], near(0, True)),
        halo(5, c_ext.at[0:2, pl.ds(0, W)], c_ext.at[T : T + 2, pl.ds(2 * W, W)], near(-1, True)),
    ])
    put_kernels(raw_first, padded, w_first, b_first)
    put_stats(0, 1, *join_stats(0, 0, stats, True))
    stats = send_stats(0, 1)
    for half in range(2):
        both = c_field[2 * half : 2 * half + 2].reshape(4 * W, L)
        gtc[:, half * 4 * W : half * 4 * W + 4 * W] = transposed(both)
    for tap in range(9):
        b_down[8 - tap, 0:C, 0:L] = w_down[tap, C : 2 * C, :]
        b_down[8 - tap, 0:C, L : 2 * L] = jnp.zeros((C, L), BF16)
        b_down[8 - tap, C : 2 * C, 0:L] = w_down[tap, 2 * C : 3 * C, :]
        b_down[8 - tap, C : 2 * C, L : 2 * L] = w_down[tap, 0:C, :]
    ends(cot_halo)

    @pl.loop(0, T + 2)
    def _(f):
        late = jnp.where(f >= T, has_next, one)
        for r in range(3):
            value = c_ext[f, r * W : (r + 1) * W, :].astype(F32) * (late * has_below if r == 2 else late)
            row = lax.broadcasted_iota(jnp.int32, (W, L), 0)
            after = jnp.where(row == W - 1, 0.0, pltpu.roll(value, W - 1, 0))
            c_win[f, r * W : (r + 1) * W, 0:L] = value.astype(BF16)
            c_win[f, r * W : (r + 1) * W, L : 2 * L] = after.astype(BF16)

    @pl.loop(0, T)
    def _(t):
        even = odd = None
        for j in range(3):
            here = c_win[t + j, 0 : 2 * W, :]
            below = c_win[t + j, W : 3 * W, :]
            a = dot_turned(here, b_down[j * 3 + 1])
            b = dot_turned(here, b_down[j * 3])
            b = b + dot_turned(below, b_down[j * 3 + 2])
            even, odd = (a, b) if j == 0 else (even + a, odd + b)
        for i in range(2):
            for parity, value in ((0, even), (1, odd)):
                r = 2 * i + parity
                piece = value[i * W : (i + 1) * W]
                g_block[t, r * W : (r + 1) * W, :] = piece
                g_ext[t, (r + 1) * W : (r + 2) * W, :] = piece.astype(BF16)

    grad_halo = begins([
        halo(6, g_ext.at[0:2, own], g_ext.at[T : T + 2, own], near(-1, False)),
        halo(7, g_ext.at[0:T, pl.ds(edge, W)], g_ext.at[0:T, pl.ds(far, W)], near(0, True)),
        halo(8, g_ext.at[0:2, pl.ds(edge, W)], g_ext.at[T : T + 2, pl.ds(far, W)], near(-1, True)),
    ])
    centre_one, scale_one = scale_of(*join_stats(0, 1, stats, True))
    ends(video_halo)

    @pl.loop(0, T + 2)
    def _(f):
        early = jnp.where(f < 2, has_past, one)
        for r in range(R + 2):
            normed = (v_ext[f, r * W : (r + 1) * W, :].astype(F32) - centre_one) * scale_one
            put_windows(win_first, f, r, normed * sigmoid(normed) * (early * row_mask(r)))

    def first_conv(t, total):
        hidden = conv(win_first, w_first, t, dot_turned).astype(BF16)
        h_ext[t + 2, W : (R + 1) * W, :] = hidden
        return total + jnp.sum(hidden.astype(F32), axis=0, keepdims=True)

    mean = lax.fori_loop(0, T, first_conv, jnp.zeros((1, L), F32)) * (1.0 / CELLS)

    def own_hidden(t):
        return h_ext[t + 2, W : (R + 1) * W, :].astype(F32)

    put_stats(1, 0, mean, spread_of(mean, own_hidden))
    stats = send_stats(1, 0)
    hidden_halo = begins([
        halo(9, h_ext.at[T : T + 2, own], h_ext.at[0:2, own], near(1, False)),
        halo(10, h_ext.at[2 : T + 2, pl.ds(edge, W)], h_ext.at[2 : T + 2, pl.ds(far, W)], near(0, True)),
        halo(11, h_ext.at[T : T + 2, pl.ds(edge, W)], h_ext.at[0:2, pl.ds(far, W)], near(1, True)),
        halo(12, h_ext.at[2:4, own], h_ext.at[T + 2 : T + 4, own], near(-1, False)),
        halo(13, h_ext.at[2:4, pl.ds(edge, W)], h_ext.at[T + 2 : T + 4, pl.ds(far, W)], near(-1, True)),
    ])

    put_kernels(raw_second, padded, w_second, b_second)
    ends(grad_halo)

    @pl.loop(0, T + 2)
    def _(f):
        late = jnp.where(f >= T, has_next, one)
        for r in range(R + 2):
            value = g_ext[f, r * W : (r + 1) * W, :].astype(F32) * (late * row_mask(r))
            put_windows(win_back, f, r, value)

    put_stats(1, 1, *join_stats(1, 0, stats, True))
    stats = send_stats(1, 1)

    @pl.loop(0, T)
    def _(t):
        t2_ext[t, W : (R + 1) * W, :] = conv(win_back, b_second, t, dot)

    act_halo = begins([
        halo(14, t2_ext.at[0:2, own], t2_ext.at[T : T + 2, own], near(-1, False)),
        halo(15, t2_ext.at[0:T, pl.ds(edge, W)], t2_ext.at[0:T, pl.ds(far, W)], near(0, True)),
        halo(16, t2_ext.at[0:2, pl.ds(edge, W)], t2_ext.at[T : T + 2, pl.ds(far, W)], near(-1, True)),
    ])

    for half in range(2):
        both = g_ext[2 * half : 2 * half + 2, W : (R + 1) * W, :].reshape(8 * W, L)
        gt[:, half * 8 * W : (half + 1) * 8 * W] = transposed(both.astype(F32))

    centre_two, scale_two = scale_of(*join_stats(1, 1, stats, True))

    def gradient(grad, normed):
        sigma = sigmoid(normed)
        return grad * sigma * (1.0 + normed * (1.0 - sigma))

    def second_sums(t, sums):
        first, second = sums
        for r in range(1, R + 1):
            normed = (h_ext[t + 2, r * W : (r + 1) * W, :].astype(F32) - centre_two) * scale_two
            grad = gradient(t2_ext[t, r * W : (r + 1) * W, :], normed)
            first = first + jnp.sum(grad, axis=0, keepdims=True)
            second = second + jnp.sum(grad * normed, axis=0, keepdims=True)
        return first, second

    nothing = (jnp.zeros((1, L), F32), jnp.zeros((1, L), F32))
    put_stats(2, 0, *lax.fori_loop(0, T, second_sums, nothing))
    stats = send_stats(2, 0)
    ends(hidden_halo)

    @pl.loop(0, T + 2)
    def _(f):
        early = jnp.where(f < 2, has_past, one)
        for r in range(R + 2):
            normed = (h_ext[f, r * W : (r + 1) * W, :].astype(F32) - centre_two) * scale_two
            put_windows(win_second, f, r, normed * sigmoid(normed) * (early * row_mask(r)))

    put_stats(2, 1, *join_stats(2, 0, stats, False))
    stats = send_stats(2, 1)

    @pl.loop(0, T)
    def _(t):
        block = v_ext[t + 2, W : (R + 1) * W, :].astype(F32) + conv(win_second, w_second, t, dot_turned)
        b_ext[t + 2, W : (R + 1) * W, :] = block.astype(BF16)

    block_halo = begins([
        halo(17, b_ext.at[T : T + 2, own], b_ext.at[0:2, own], near(1, False)),
        halo(18, b_ext.at[2 : T + 2, pl.ds(R * W, W)], b_ext.at[2 : T + 2, pl.ds(0, W)], near(0, True)),
        halo(19, b_ext.at[T : T + 2, pl.ds(R * W, W)], b_ext.at[0:2, pl.ds(0, W)], near(1, True)),
    ])

    def block_weights(windows, full):
        left = lanes((C, L)) < C

        def folded(tap):
            dt, dr = tap // 3, tap % 3
            cells = windows[dt : dt + T, dr * W : (dr + R) * W, :].reshape(CELLS, 2 * L)
            both = dot(gt[...], cells)
            return both[0:C] + pltpu.roll(both[C : 2 * C], 3 * C, 1)

        def put(tile, value):
            full[tile * C : (tile + 1) * C, :] = value

        for pair in range(4):
            a, b = folded(2 * pair), pltpu.roll(folded(2 * pair + 1), C, 1)
            put(3 * pair, a[:, 0:L])
            put(3 * pair + 1, jnp.where(left, a[:, L : 2 * L], b[:, 0:L]))
            put(3 * pair + 2, b[:, L : 2 * L])
        value = folded(8)
        put(12, value[:, 0:L])
        put(13, jnp.where(left, value[:, L : 2 * L], 0.0))

    full_sd[HALF + 27 * C :, :] = jnp.zeros((full_sd.shape[0] - HALF - 27 * C, L), F32)
    full_f[HALF:, :] = jnp.zeros((full_f.shape[0] - HALF, L), F32)
    block_weights(win_second, full_sd)

    ends(block_halo)

    @pl.loop(0, T + 2)
    def _(f):
        early = jnp.where(f < 2, has_past, one)
        for r in range(R + 1):
            value = b_ext[f, r * W : (r + 1) * W, :].astype(F32) * (early * has_above if r == 0 else early)
            put_windows(b_odd if r % 2 else b_even, f, r // 2, value)

    def projected(dr):
        return (b_even, 0) if dr == 0 else (b_odd, 0) if dr == 1 else (b_even, W)

    for dt in range(3):
        for dr in range(3):
            ref, start = projected(dr)
            cells = ref[dt : dt + T, start : start + 2 * W, :].reshape(2 * W * T, 2 * L)
            turned = jnp.dot(gtc[...], cells, preferred_element_type=F32).T
            base = HALF + (dt * 3 + dr) * 3 * C
            full_sd[base : base + 3 * C, :] = turned[0 : 3 * C]

    class Reduction:
        def __init__(self, number, piece, full, send, recv, sums, recvb, whole):
            self.n, self.piece = number, piece
            self.full, self.send, self.recv, self.sums = full, send, recv, sums
            self.recvb, self.whole = recvb, whole

        def sem(self, sems, k):
            return sems.at[0, self.n, k], sems.at[1, self.n, k]

        def part(self, index):
            return pl.ds(pl.multiple_of(index * self.piece, 16), self.piece)

        def start(self):
            self.send[...] = self.full[...].astype(BF16)
            self.copies = begins([
                remote(
                    self.send.at[self.part(lax.rem(plane + k, PLANE))], self.recv.at[k - 1],
                    *self.sem(wa_sems, k), plane_peer(k),
                )
                for k in range(1, PLANE)
            ])

        def second(self):
            ends(self.copies)
            value = self.full[self.part(plane), :]
            for k in range(PLANE - 1):
                value = value + self.recv[k].astype(F32)
            self.sums[...] = value
            self.copies = begins([
                remote(self.sums, self.recvb.at[column], *self.sem(wb_sems, k), column_peer(k))
                for k in range(1, COLUMN)
            ])
            self.recvb[column] = value

        def third(self):
            ends(self.copies)
            value = self.recvb[0]
            for k in range(1, COLUMN):
                value = value + self.recvb[k]
            value = value * (1.0 / math.sqrt(2 * 128 * 8 * 160))
            here = self.part(plane)
            self.whole[here, :] = value.astype(BF16)
            self.copies = begins([
                remote(self.whole.at[here], self.whole.at[here], *self.sem(wc_sems, k), plane_peer(k))
                for k in range(1, PLANE)
            ])

        def finish(self):
            ends(self.copies)

    sums_sd = Reduction(0, PIECE_SD, full_sd, send_sd, recv_sd, sum_sd, recvb_sd, all_sd)
    sums_f = Reduction(1, PIECE_F, full_f, send_f, recv_f, sum_f, recvb_f, all_f)
    sums_sd.start()

    count = 1.0 / (4 * GROUP_CELLS)
    ends(act_halo)
    first, second = join_stats(2, 1, stats, False)
    mean_one, mean_two = over_group(first) * count, over_group(second) * count

    @pl.loop(0, T + 2)
    def _(f):
        late = jnp.where(f >= T, has_next, one)
        for r in range(R + 2):
            normed = (h_ext[f + 2, r * W : (r + 1) * W, :].astype(F32) - centre_two) * scale_two
            grad = gradient(t2_ext[f, r * W : (r + 1) * W, :], normed)
            hidden = scale_two * (grad - mean_one - normed * mean_two)
            put_windows(win_back, f, r, hidden * (late * row_mask(r)))
            if 1 <= r <= R:

                @pl.when(f < T)
                def _():
                    field[f, (r - 1) * W : r * W, :] = hidden

    for half in range(2):
        both = field[2 * half : 2 * half + 2].reshape(8 * W, L)
        gt[:, half * 8 * W : (half + 1) * 8 * W] = transposed(both)
    block_weights(win_first, full_f)
    sums_f.start()
    sums_sd.second()

    def back_first(t, sums):
        back = conv(win_back, b_first, t, dot)
        normed = (v_ext[t + 2, W : (R + 1) * W, :].astype(F32) - centre_one) * scale_one
        grad = gradient(back, normed)
        t1[t] = grad
        return (
            sums[0] + jnp.sum(grad, axis=0, keepdims=True),
            sums[1] + jnp.sum(grad * normed, axis=0, keepdims=True),
        )

    put_stats(3, 0, *lax.fori_loop(0, T, back_first, nothing))
    stats = send_stats(3, 0)
    sums_f.second()

    @pl.loop(0, T)
    def _(t):
        total = None
        for dt in range(3):
            for dr in range(3):
                ref, start = projected(dr)
                part = dot(ref[t + dt, start : start + 2 * W, 0 : 3 * C], w_down[dt * 3 + dr])
                total = part if total is None else total + part
        out_down[t] = total

    put_stats(3, 1, *join_stats(3, 0, stats, False))
    stats = send_stats(3, 1)
    sums_sd.third()
    sums_f.third()
    first, second = join_stats(3, 1, stats, False)
    mean_one, mean_two = over_group(first) * count, over_group(second) * count

    @pl.loop(0, T)
    def _(t):
        normed = (v_ext[t + 2, W : (R + 1) * W, :].astype(F32) - centre_one) * scale_one
        out_video[t] = g_block[t] + scale_one * (t1[t] - mean_one - normed * mean_two)

    sums_sd.finish()
    sums_f.finish()


def finish_kernel(down, video, sums_sd, sums_f, out_down, out_video, out_first, out_second, out_grad_down):
    for p in range(W):
        here = slice(p * L, (p + 1) * L)
        out_video[0, 0, :, here] = video[0, pl.ds(p, R, stride=W), :]
        out_down[0, 0, :, here] = down[0, pl.ds(p, 2, stride=W), :].astype(BF16)

    @pl.when(pl.program_id(0) == 0)
    def _():
        for source, target in ((sums_sd, out_second), (sums_f, out_first)):
            for tile in range(TILES):
                width = min(L, 27 * C - tile * L)
                value = source[tile * C : (tile + 1) * C, :].astype(F32)
                target[:, tile * L : tile * L + width] = value[:, 0:width]
        out_grad_down[...] = sums_sd[HALF : HALF + 27 * C, :].astype(F32)


def local(video, conv_first, conv_second, conv_down, down_cotangent):
    operands = (
        video, down_cotangent, conv_first.T, conv_second.T, conv_down.reshape(9, 3 * C, C_OUT)
    )
    rows = (R + 2) * W

    def reduction(piece):
        return [
            pltpu.VMEM((piece * PLANE, L), F32),
            pltpu.VMEM((piece * PLANE, L), BF16),
            pltpu.VMEM((PLANE - 1, piece, L), BF16),
            pltpu.VMEM((piece, L), F32),
            pltpu.VMEM((COLUMN, piece, L), F32),
        ]

    vmem = pl.BlockSpec(memory_space=pltpu.VMEM)
    dma = pltpu.SemaphoreType.DMA
    results = pl.pallas_call(
        kernel,
        out_shape=(
            jax.ShapeDtypeStruct((T, 2 * W, L), F32),
            jax.ShapeDtypeStruct((T, R * W, L), F32),
            jax.ShapeDtypeStruct((PIECE_SD * PLANE, L), BF16),
            jax.ShapeDtypeStruct((PIECE_F * PLANE, L), BF16),
        ),
        in_specs=[vmem] * len(operands),
        out_specs=(vmem,) * 4,
        scratch_shapes=[
            pltpu.VMEM((C, TILES * L), F32),
            pltpu.VMEM((9, 2 * C, 4 * C), BF16),
            pltpu.VMEM((9, 2 * C, 4 * C), BF16),
            pltpu.VMEM((9, 4 * C, 2 * C), BF16),
            pltpu.VMEM((9, 4 * C, 2 * C), BF16),
            pltpu.VMEM((9, 2 * C, 2 * C_OUT), BF16),
            pltpu.VMEM((T + 2, rows, L), BF16),
            pltpu.VMEM((T, R * W, L), F32),
            pltpu.VMEM((T + 2, 3 * W, L), BF16),
            pltpu.VMEM((T, 2 * W, L), F32),
            pltpu.VMEM((T + 2, 3 * W, 2 * L), BF16),
            pltpu.VMEM((T, R * W, L), F32),
            pltpu.VMEM((T + 2, rows, L), BF16),
            pltpu.VMEM((T + 4, rows, L), BF16),
            pltpu.VMEM((T + 2, rows, L), F32),
            pltpu.VMEM((T, R * W, L), F32),
            pltpu.VMEM((T + 2, rows, 2 * L), BF16),
            pltpu.VMEM((T + 2, rows, 2 * L), BF16),
            pltpu.VMEM((T + 2, rows, 2 * L), BF16),
            pltpu.VMEM((T + 2, (R + 1) * W, L), BF16),
            pltpu.VMEM((T + 2, 3 * W, 2 * L), BF16),
            pltpu.VMEM((T + 2, 2 * W, 2 * L), BF16),
            pltpu.VMEM((L, CELLS), BF16),
            pltpu.VMEM((L, CELLS // 2), BF16),
            pltpu.VMEM((4, 2, 8, L), F32),
            pltpu.VMEM((4, 2, LOW, 8, L), F32),
            *reduction(PIECE_SD),
            *reduction(PIECE_F),
            dma((2, 20)),
            dma((2, 4, 2, LOW)),
            dma((2, 2, PLANE)),
            dma((2, 2, COLUMN)),
            dma((2, 2, PLANE)),
        ],
        compiler_params=pltpu.CompilerParams(
            collective_id=1, has_side_effects=True, vmem_limit_bytes=56 * 1024 * 1024
        ),
    )(*operands)

    def frame(*shape):
        return pl.BlockSpec(shape, lambda t: (t,) + (0,) * (len(shape) - 1))

    def out_frame(rows):
        return pl.BlockSpec((1, 1, rows, W * L), lambda t: (0, t, 0, 0))

    def whole(*shape):
        return pl.BlockSpec(shape, lambda t: (0,) * len(shape))

    down, grad_video, first, second, grad_down = pl.pallas_call(
        finish_kernel,
        grid=(T,),
        out_shape=(
            jax.ShapeDtypeStruct((1, T, 2, W * L), BF16),
            jax.ShapeDtypeStruct((1, T, R, W * L), F32),
            jax.ShapeDtypeStruct((C, 27 * C), F32),
            jax.ShapeDtypeStruct((C, 27 * C), F32),
            jax.ShapeDtypeStruct((27 * C, C_OUT), F32),
        ),
        in_specs=[
            frame(1, 2 * W, L),
            frame(1, R * W, L),
            whole(PIECE_SD * PLANE, L),
            whole(PIECE_F * PLANE, L),
        ],
        out_specs=(
            out_frame(2), out_frame(R), whole(C, 27 * C), whole(C, 27 * C), whole(27 * C, C_OUT)
        ),
        compiler_params=pltpu.CompilerParams(vmem_limit_bytes=32 * 1024 * 1024),
    )(*results)
    return down, grad_video, first.T, second.T, grad_down


def solution(mesh):
    in_specs = (P("clip", "tm", "space", None), P(), P(), P(), P("clip", "tm", "space", None))
    out_specs = (P("clip", "tm", "space", None), P("clip", "tm", "space", None), P(), P(), P())
    return jax.shard_map(local, mesh=mesh, in_specs=in_specs, out_specs=out_specs, check_vma=False)
```

```python
import functools
import math

import jax
import jax.numpy as jnp
from jax import lax
from jax.experimental import pallas as pl
from jax.experimental.pallas import tpu as pltpu
from jax.sharding import PartitionSpec as P

MESH = pl.DeviceIdType.MESH
F32 = jnp.float32
BF16 = jnp.bfloat16
EPSILON = 1e-06
C = 64
C_OUT = 128
T = 4
R = 4
W = 80
L = 128
TM = 32
LOW = 8
HIGH = 8
PLANE = 16
COLUMN = 8
PIECE_SD = 176
PIECE_F = 64
TILES = 14
HALF = TILES * C
CELLS = T * R * W
GROUP_CELLS = CELLS * 64


def low_peer(step):
    tm = lax.axis_index("tm")
    low = lax.rem(tm, LOW)
    return {"tm": tm - low + lax.rem(low + step, LOW)}


def high_peer(step):
    tm, space = lax.axis_index("tm"), lax.axis_index("space")
    place = lax.rem((tm // LOW) * 2 + space + step, HIGH)
    return {"tm": (place // 2) * LOW + lax.rem(tm, LOW), "space": lax.rem(place, 2)}


def plane_place():
    return lax.axis_index("tm") // 2


def plane_peer(step):
    tm = lax.axis_index("tm")
    return {"tm": lax.rem(tm // 2 + step, PLANE) * 2 + lax.rem(tm, 2)}


def column_place():
    core = lax.rem(lax.axis_index("tm"), 2)
    return (core * 2 + lax.axis_index("space")) * 2 + lax.axis_index("clip")


def column_peer(step):
    tm = lax.axis_index("tm")
    place = lax.rem(column_place() + step, COLUMN)
    return {
        "tm": (tm // 2) * 2 + place // 4,
        "space": lax.rem(place // 2, 2),
        "clip": lax.rem(place, 2),
    }


def near(step, across):
    tm, space = lax.axis_index("tm"), lax.axis_index("space")
    device = {}
    if step:
        device["tm"] = lax.rem(tm + step + TM, TM)
    if across:
        device["space"] = 1 - space
    return device


def ends(copies):
    for copy in copies:
        copy.wait()


def begins(copies):
    for copy in copies:
        copy.start()
    return copies


def lanes(shape):
    return lax.broadcasted_iota(jnp.int32, shape, len(shape) - 1)


def over_group(value):
    wide = jnp.broadcast_to(value, (8, L))
    both = wide + pltpu.roll(wide, C, 1)
    even = lax.rem(lanes((8, L)), 2) == 0
    other = jnp.where(even, pltpu.roll(both, L - 1, 1), pltpu.roll(both, 1, 1))
    return (both + other)[0:1]


def put_windows(target, f, r, x):
    turned = pltpu.roll(x, C, 1)
    row = lax.broadcasted_iota(jnp.int32, (W, L), 0)
    left = lanes((W, L)) < C
    above = jnp.where(row == 0, 0.0, pltpu.roll(turned, 1, 0))
    below = jnp.where(row == W - 1, 0.0, pltpu.roll(turned, W - 1, 0))
    target[f, r * W : (r + 1) * W, 0:L] = jnp.where(left, above, turned).astype(BF16)
    target[f, r * W : (r + 1) * W, L : 2 * L] = jnp.where(left, turned, below).astype(BF16)


def dot_turned(a, b):
    return lax.dot_general(a, b, (((1,), (1,)), ((), ())), preferred_element_type=F32)


def dot(a, b):
    return jnp.dot(a, b, preferred_element_type=F32)


def conv(windows, weights, total, multiply):
    total[...] = jnp.zeros_like(total)

    @pl.loop(0, 4)
    def _(o):
        value = None
        for dr in range(3):
            rows = slice(dr * W, (dr + R) * W)
            both = jnp.concatenate([windows[o, rows, :], windows[o + 2, rows, :]], axis=0)
            part = multiply(both, weights[o, dr])
            value = part if value is None else value + part
        total[...] = total[...] + value


def put_kernels(raw, padded, ahead, back):
    width = 27 * C
    padded[:, 0:width] = raw[...].astype(F32)
    padded[:, width:] = jnp.zeros((C, padded.shape[1] - width), F32)
    lane = lanes((C, 4 * C))
    for dr in range(3):
        ahead[0, dr, 2 * C : 4 * C, :] = jnp.zeros((2 * C, 4 * C), BF16)
        ahead[3, dr, 0 : 2 * C, :] = jnp.zeros((2 * C, 4 * C), BF16)
        back[0, dr, :, 2 * C : 4 * C] = jnp.zeros((4 * C, 2 * C), BF16)
        back[3, dr, :, 0 : 2 * C] = jnp.zeros((4 * C, 2 * C), BF16)
    for tap in range(9):
        start = tap * 3 * C
        if tap % 2 == 0:
            near = jnp.where(lane < 3 * C, padded[:, start : start + 4 * C], 0.0)
            later = pltpu.roll(near, C, 1)
        else:
            later = jnp.where(lane < C, 0.0, padded[:, start - C : start + 3 * C])
            near = pltpu.roll(later, 3 * C, 1)
        near, later = near.astype(BF16), later.astype(BF16)
        dt, dr = tap // 3, tap % 3
        for frame in range(2):
            base = frame * 2 * C
            ahead[dt + frame, dr, base : base + C, :] = near
            ahead[dt + frame, dr, base + C : base + 2 * C, :] = later
            target = back.at[2 - dt + frame, 2 - dr]
            here = slice(base, base + 2 * C)
            target[0:C, here] = near[:, 2 * C :]
            target[C : 2 * C, here] = later[:, 2 * C :]
            target[2 * C : 3 * C, here] = near[:, 0 : 2 * C]
            target[3 * C : 4 * C, here] = later[:, 0 : 2 * C]


def sigmoid(value):
    return 0.5 + 0.5 * jnp.tanh(0.5 * value)


def transposed(source):
    return source.T.astype(BF16)


def kernel(
    video, cot, raw_first, raw_second, w_down,
    out_down, out_video, all_sd, all_f,
    padded, w_first, w_second, b_first, b_second, b_down, wide,
    v_ext, field, c_ext, c_field, c_win, g_block, h_ext, t2_ext, t2, t1, win_first, win_second,
    win_back, b_ext, b_even, b_odd, gt, gtc, st_src, st_buf,
    full_sd, send_sd, recv_sd, sum_sd, recvb_sd,
    full_f, send_f, recv_f, sum_f, recvb_f,
    halo_sems, st_sems, wa_sems, wb_sems, wc_sems,
):
    tm, space = lax.axis_index("tm"), lax.axis_index("space")
    low = lax.rem(tm, LOW)
    high = (tm // LOW) * 2 + space
    plane, column = plane_place(), column_place()
    has_past = jnp.where(tm == 0, 0.0, 1.0).astype(F32)
    has_next = jnp.where(tm == TM - 1, 0.0, 1.0).astype(F32)
    has_above = jnp.where(space == 0, 0.0, 1.0).astype(F32)
    has_below = jnp.where(space == 1, 0.0, 1.0).astype(F32)
    one = jnp.ones((), F32)

    def row_mask(r):
        return has_above if r == 0 else has_below if r == R + 1 else one

    edge = pl.multiple_of((R - (R - 1) * space) * W, W)
    far = pl.multiple_of((R + 1) * space * W, W)

    peers = [low_peer(k) for k in range(1, LOW)] + [high_peer(k) for k in range(1, HIGH)]
    peers += [plane_peer(k) for k in range(1, PLANE)] + [column_peer(k) for k in range(1, COLUMN)]
    peers += [near(1, False), near(-1, False), near(1, True), near(-1, True)]
    barrier = pltpu.get_barrier_semaphore()
    for peer in peers:
        pl.semaphore_signal(barrier, inc=1, device_id=peer, device_id_type=MESH)

    def remote(source, target, send, recv, device):
        return pltpu.make_async_remote_copy(
            src_ref=source, dst_ref=target, send_sem=send, recv_sem=recv,
            device_id=device, device_id_type=MESH,
        )

    def halo(slot, source, target, device):
        return remote(source, target, halo_sems.at[0, slot], halo_sems.at[1, slot], device)

    def send_stats(k, stage):
        me, peer, size = (high, high_peer, HIGH) if stage == 0 else (low, low_peer, LOW)
        copies = begins([
            remote(
                st_src.at[k, stage], st_buf.at[k, stage, me],
                st_sems.at[0, k, stage, j], st_sems.at[1, k, stage, j], peer(j),
            )
            for j in range(1, size)
        ])
        st_buf[k, stage, me] = st_src[k, stage]
        return copies

    def join_stats(k, stage, copies, centred):
        ends(copies)
        parts = [st_buf[k, stage, j] for j in range(LOW)]
        total = parts[0]
        for part in parts[1:]:
            total = total + part
        first, second = total[0:1], total[1:2]
        if centred:
            cells = float(CELLS * (1 if stage == 0 else LOW))
            first = first * (1.0 / LOW)
            for part in parts:
                second = second + cells * ((part[0:1] - first) * (part[0:1] - first))
        return first, second

    def put_stats(k, stage, first, second):
        st_src[k, stage] = jnp.zeros((8, L), F32)
        st_src[k, stage, 0:1] = first
        st_src[k, stage, 1:2] = second

    def scale_of(mean, spread):
        centre = over_group(mean) * 0.25
        gap = mean - centre
        variance = over_group(spread + float(GROUP_CELLS) * (gap * gap)) * (1.0 / (4 * GROUP_CELLS))
        return centre, lax.rsqrt(variance + EPSILON)

    def spread_of(mean, read):
        def step(t, total):
            gap = read(t) - mean
            return total + jnp.sum(gap * gap, axis=0, keepdims=True)

        return lax.fori_loop(0, T, step, jnp.zeros((1, L), F32))

    def take_video(t, total):
        for p in range(W):
            field[t, pl.ds(p, R, stride=W), :] = video[0, t, :, p * L : (p + 1) * L].astype(F32)
        value = field[t]
        v_ext[t + 2, W : (R + 1) * W, :] = value.astype(BF16)
        return total + jnp.sum(value, axis=0, keepdims=True)

    mean = lax.fori_loop(0, T, take_video, jnp.zeros((1, L), F32)) * (1.0 / CELLS)
    put_stats(0, 0, mean, spread_of(mean, lambda t: field[t]))
    pl.semaphore_wait(barrier, len(peers))
    stats = send_stats(0, 0)
    own = pl.ds(W, R * W)
    video_halo = begins([
        halo(0, v_ext.at[T : T + 2, own], v_ext.at[0:2, own], near(1, False)),
        halo(1, v_ext.at[2 : T + 2, pl.ds(edge, W)], v_ext.at[2 : T + 2, pl.ds(far, W)], near(0, True)),
        halo(2, v_ext.at[T : T + 2, pl.ds(edge, W)], v_ext.at[0:2, pl.ds(far, W)], near(1, True)),
    ])
    for ref in (v_ext, h_ext, t2_ext):
        for f in range(ref.shape[0]):
            ref[f, pl.ds(far, W), :] = jnp.zeros((W, L), ref.dtype)

    @pl.loop(0, T)
    def _(t):
        for p in range(W):
            c_field[t, pl.ds(p, 2, stride=W), :] = cot[0, t, :, p * L : (p + 1) * L].astype(F32)
        c_ext[t, W : 3 * W, :] = c_field[t].astype(BF16)

    c_own = pl.ds(W, 2 * W)
    c_edge = pl.ds(pl.multiple_of((2 - space) * W, W), W)
    c_far = pl.ds(pl.multiple_of(3 * space * W, W), W)
    cot_halo = begins([
        halo(3, c_ext.at[0:T, c_own], c_ext.at[T : 2 * T, c_own], near(-1, False)),
        halo(4, c_ext.at[0:T, c_edge], c_ext.at[0:T, c_far], near(0, True)),
        halo(5, c_ext.at[0:T, c_edge], c_ext.at[T : 2 * T, c_far], near(-1, True)),
    ])
    for f in range(2 * T):
        c_ext[f, c_far, :] = jnp.zeros((W, L), BF16)
    put_kernels(raw_first, padded, w_first, b_first)
    put_stats(0, 1, *join_stats(0, 0, stats, True))
    stats = send_stats(0, 1)
    for half in range(2):
        both = c_field[2 * half : 2 * half + 2].reshape(4 * W, L)
        gtc[:, half * 4 * W : half * 4 * W + 4 * W] = transposed(both)
    for tap in range(9):
        b_down[8 - tap, 0:C, 0:L] = w_down[tap, C : 2 * C, :]
        b_down[8 - tap, 0:C, L : 2 * L] = jnp.zeros((C, L), BF16)
        b_down[8 - tap, C : 2 * C, 0:L] = w_down[tap, 2 * C : 3 * C, :]
        b_down[8 - tap, C : 2 * C, L : 2 * L] = w_down[tap, 0:C, :]
    ends(cot_halo)

    @pl.loop(0, 2 * T)
    def _(f):
        late = jnp.where(f >= T, has_next, one)
        row = lax.broadcasted_iota(jnp.int32, (W, L), 0)
        for r in range(4):
            value = c_ext[f, r * W : (r + 1) * W, :].astype(F32)
            value = value * (late * has_above if r == 0 else late * has_below if r == 3 else late)
            after = jnp.where(row == W - 1, 0.0, pltpu.roll(value, W - 1, 0))
            c_win[f, r * W : (r + 1) * W, 0:L] = value.astype(BF16)
            c_win[f, r * W : (r + 1) * W, L : 2 * L] = after.astype(BF16)

    @pl.loop(0, T + 2)
    def _(f):
        late = jnp.where(f >= T, has_next, one)
        even = odd = None
        for j in range(3):
            upper = c_win[f + j, 0 : 3 * W, :]
            lower = c_win[f + j, W : 4 * W, :]
            a = dot_turned(lower, b_down[j * 3 + 1])
            b = dot_turned(upper, b_down[j * 3])
            b = b + dot_turned(lower, b_down[j * 3 + 2])
            even, odd = (a, b) if j == 0 else (even + a, odd + b)
        for i in range(3):
            for r, value in ((2 * i, odd), (2 * i + 1, even)):
                put_windows(win_back, f, r, value[i * W : (i + 1) * W] * (late * row_mask(r)))

        @pl.when(f < T)
        def _():
            for r in range(1, R + 1):
                value = (even if r % 2 else odd)[(r // 2) * W : (r // 2 + 1) * W]
                g_block[f, (r - 1) * W : r * W, :] = value

    centre_one, scale_one = scale_of(*join_stats(0, 1, stats, True))
    ends(video_halo)

    @pl.loop(0, T + 2)
    def _(f):
        early = jnp.where(f < 2, has_past, one)
        for r in range(R + 2):
            normed = (v_ext[f, r * W : (r + 1) * W, :].astype(F32) - centre_one) * scale_one
            put_windows(win_first, f, r, normed * sigmoid(normed) * (early * row_mask(r)))

    def result(q, frame):
        here = slice(frame * L, (frame + 1) * L)
        return wide[q * R * W : (q + 1) * R * W, here]

    def frames_of(step, start):
        for q in range(T // 2):
            for frame in range(2):
                start = step(2 * q + frame, result(q, frame), start)
        return start

    def first_conv(t, value, total):
        hidden = value.astype(BF16)
        h_ext[t + 2, W : (R + 1) * W, :] = hidden
        return total + jnp.sum(hidden.astype(F32), axis=0, keepdims=True)

    conv(win_first, w_first, wide, dot_turned)
    mean = frames_of(first_conv, jnp.zeros((1, L), F32)) * (1.0 / CELLS)

    def own_hidden(t):
        return h_ext[t + 2, W : (R + 1) * W, :].astype(F32)

    put_stats(1, 0, mean, spread_of(mean, own_hidden))
    stats = send_stats(1, 0)
    hidden_halo = begins([
        halo(9, h_ext.at[T : T + 2, own], h_ext.at[0:2, own], near(1, False)),
        halo(10, h_ext.at[2 : T + 2, pl.ds(edge, W)], h_ext.at[2 : T + 2, pl.ds(far, W)], near(0, True)),
        halo(11, h_ext.at[T : T + 2, pl.ds(edge, W)], h_ext.at[0:2, pl.ds(far, W)], near(1, True)),
        halo(12, h_ext.at[2:4, own], h_ext.at[T + 2 : T + 4, own], near(-1, False)),
        halo(13, h_ext.at[2:4, pl.ds(edge, W)], h_ext.at[T + 2 : T + 4, pl.ds(far, W)], near(-1, True)),
    ])

    put_kernels(raw_second, padded, w_second, b_second)
    for half in range(2):
        both = g_block[2 * half : 2 * half + 2].reshape(8 * W, L)
        gt[:, half * 8 * W : (half + 1) * 8 * W] = transposed(both)

    put_stats(1, 1, *join_stats(1, 0, stats, True))
    stats = send_stats(1, 1)

    def keep_back(t, value, _):
        t2[t] = value
        t2_ext[t, W : (R + 1) * W, :] = value.astype(BF16)

    conv(win_back, b_second, wide, dot)
    frames_of(keep_back, None)

    act_halo = begins([
        halo(14, t2_ext.at[0:2, own], t2_ext.at[T : T + 2, own], near(-1, False)),
        halo(15, t2_ext.at[0:T, pl.ds(edge, W)], t2_ext.at[0:T, pl.ds(far, W)], near(0, True)),
        halo(16, t2_ext.at[0:2, pl.ds(edge, W)], t2_ext.at[T : T + 2, pl.ds(far, W)], near(-1, True)),
    ])

    centre_two, scale_two = scale_of(*join_stats(1, 1, stats, True))

    def gradient(grad, normed):
        sigma = sigmoid(normed)
        return grad * sigma * (1.0 + normed * (1.0 - sigma))

    def second_sums(t, sums):
        first, second = sums
        for r in range(1, R + 1):
            normed = (h_ext[t + 2, r * W : (r + 1) * W, :].astype(F32) - centre_two) * scale_two
            grad = gradient(t2[t, (r - 1) * W : r * W, :], normed)
            t2[t, (r - 1) * W : r * W, :] = grad
            first = first + jnp.sum(grad, axis=0, keepdims=True)
            second = second + jnp.sum(grad * normed, axis=0, keepdims=True)
        return first, second

    nothing = (jnp.zeros((1, L), F32), jnp.zeros((1, L), F32))
    put_stats(2, 0, *lax.fori_loop(0, T, second_sums, nothing))
    stats = send_stats(2, 0)
    ends(hidden_halo)

    @pl.loop(0, T + 2)
    def _(f):
        early = jnp.where(f < 2, has_past, one)
        for r in range(R + 2):
            normed = (h_ext[f, r * W : (r + 1) * W, :].astype(F32) - centre_two) * scale_two
            put_windows(win_second, f, r, normed * sigmoid(normed) * (early * row_mask(r)))

    put_stats(2, 1, *join_stats(2, 0, stats, False))
    stats = send_stats(2, 1)

    def add_input(t, value, _):
        block = v_ext[t + 2, W : (R + 1) * W, :].astype(F32) + value
        b_ext[t + 2, W : (R + 1) * W, :] = block.astype(BF16)

    conv(win_second, w_second, wide, dot_turned)
    frames_of(add_input, None)

    block_halo = begins([
        halo(17, b_ext.at[T : T + 2, own], b_ext.at[0:2, own], near(1, False)),
        halo(18, b_ext.at[2 : T + 2, pl.ds(R * W, W)], b_ext.at[2 : T + 2, pl.ds(0, W)], near(0, True)),
        halo(19, b_ext.at[T : T + 2, pl.ds(R * W, W)], b_ext.at[0:2, pl.ds(0, W)], near(1, True)),
    ])

    def block_weights(windows, full):
        left = lanes((C, L)) < C

        def folded(tap):
            dt, dr = tap // 3, tap % 3
            cells = windows[dt : dt + T, dr * W : (dr + R) * W, :].reshape(CELLS, 2 * L)
            both = dot(gt[...], cells)
            return both[0:C] + pltpu.roll(both[C : 2 * C], 3 * C, 1)

        def put(tile, value):
            full[tile * C : (tile + 1) * C, :] = value

        for pair in range(4):
            a, b = folded(2 * pair), pltpu.roll(folded(2 * pair + 1), C, 1)
            put(3 * pair, a[:, 0:L])
            put(3 * pair + 1, jnp.where(left, a[:, L : 2 * L], b[:, 0:L]))
            put(3 * pair + 2, b[:, L : 2 * L])
        value = folded(8)
        put(12, value[:, 0:L])
        put(13, jnp.where(left, value[:, L : 2 * L], 0.0))

    full_sd[HALF + 27 * C :, :] = jnp.zeros((full_sd.shape[0] - HALF - 27 * C, L), F32)
    full_f[HALF:, :] = jnp.zeros((full_f.shape[0] - HALF, L), F32)
    block_weights(win_second, full_sd)

    ends(block_halo)

    @pl.loop(0, T + 2)
    def _(f):
        early = jnp.where(f < 2, has_past, one)
        for r in range(R + 1):
            value = b_ext[f, r * W : (r + 1) * W, :].astype(F32) * (early * has_above if r == 0 else early)
            put_windows(b_odd if r % 2 else b_even, f, r // 2, value)

    def projected(dr):
        return (b_even, 0) if dr == 0 else (b_odd, 0) if dr == 1 else (b_even, W)

    for dt in range(3):
        for dr in range(3):
            ref, start = projected(dr)
            cells = ref[dt : dt + T, start : start + 2 * W, :].reshape(2 * W * T, 2 * L)
            turned = jnp.dot(gtc[...], cells, preferred_element_type=F32).T
            base = HALF + (dt * 3 + dr) * 3 * C
            full_sd[base : base + 3 * C, :] = turned[0 : 3 * C]

    class Reduction:
        def __init__(self, number, piece, full, send, recv, sums, recvb, whole):
            self.n, self.piece = number, piece
            self.full, self.send, self.recv, self.sums = full, send, recv, sums
            self.recvb, self.whole = recvb, whole

        def sem(self, sems, k):
            return sems.at[0, self.n, k], sems.at[1, self.n, k]

        def part(self, index):
            return pl.ds(pl.multiple_of(index * self.piece, 16), self.piece)

        def start(self):
            self.send[...] = self.full[...].astype(BF16)
            self.copies = begins([
                remote(
                    self.send.at[self.part(lax.rem(plane + k, PLANE))], self.recv.at[k - 1],
                    *self.sem(wa_sems, k), plane_peer(k),
                )
                for k in range(1, PLANE)
            ])

        def second(self):
            ends(self.copies)
            value = self.full[self.part(plane), :]
            for k in range(PLANE - 1):
                value = value + self.recv[k].astype(F32)
            self.sums[...] = value.astype(BF16)
            self.copies = begins([
                remote(self.sums, self.recvb.at[column], *self.sem(wb_sems, k), column_peer(k))
                for k in range(1, COLUMN)
            ])
            self.recvb[column] = value.astype(BF16)

        def third(self):
            ends(self.copies)
            value = self.recvb[0].astype(F32)
            for k in range(1, COLUMN):
                value = value + self.recvb[k].astype(F32)
            value = value * (1.0 / math.sqrt(2 * 128 * 8 * 160))
            here = self.part(plane)
            self.whole[here, :] = value.astype(BF16)
            self.copies = begins([
                remote(self.whole.at[here], self.whole.at[here], *self.sem(wc_sems, k), plane_peer(k))
                for k in range(1, PLANE)
            ])

        def finish(self):
            ends(self.copies)

    sums_sd = Reduction(0, PIECE_SD, full_sd, send_sd, recv_sd, sum_sd, recvb_sd, all_sd)
    sums_f = Reduction(1, PIECE_F, full_f, send_f, recv_f, sum_f, recvb_f, all_f)
    sums_sd.start()

    count = 1.0 / (4 * GROUP_CELLS)
    first, second = join_stats(2, 1, stats, False)
    mean_one, mean_two = over_group(first) * count, over_group(second) * count

    def hidden_row(f, r, normed, grad, mask):
        hidden = scale_two * (grad - mean_one - normed * mean_two)
        put_windows(win_back, f, r, hidden * mask)
        return hidden

    def second_normed(f, r):
        return (h_ext[f + 2, r * W : (r + 1) * W, :].astype(F32) - centre_two) * scale_two

    def far_row(f, r, mask):
        normed = second_normed(f, r)
        grad = gradient(t2_ext[f, r * W : (r + 1) * W, :].astype(F32), normed)
        hidden_row(f, r, normed, grad, mask)

    @pl.loop(0, T)
    def _(f):
        for r in range(1, R + 1):
            here = slice((r - 1) * W, r * W)
            field[f, here, :] = hidden_row(f, r, second_normed(f, r), t2[f, here, :], one)

    for half in range(2):
        both = field[2 * half : 2 * half + 2].reshape(8 * W, L)
        gt[:, half * 8 * W : (half + 1) * 8 * W] = transposed(both)
    block_weights(win_first, full_f)
    sums_f.start()
    ends(act_halo)

    @pl.loop(0, T)
    def _(f):
        for r in (0, R + 1):
            far_row(f, r, row_mask(r))

    @pl.loop(T, T + 2)
    def _(f):
        for r in range(R + 2):
            far_row(f, r, has_next * row_mask(r))

    sums_sd.second()

    def back_first(t, back, sums):
        normed = (v_ext[t + 2, W : (R + 1) * W, :].astype(F32) - centre_one) * scale_one
        grad = gradient(back, normed)
        t1[t] = grad
        return (
            sums[0] + jnp.sum(grad, axis=0, keepdims=True),
            sums[1] + jnp.sum(grad * normed, axis=0, keepdims=True),
        )

    conv(win_back, b_first, wide, dot)
    put_stats(3, 0, *frames_of(back_first, nothing))
    stats = send_stats(3, 0)
    sums_f.second()

    @pl.loop(0, T)
    def _(t):
        total = None
        for dt in range(3):
            for dr in range(3):
                ref, start = projected(dr)
                part = dot(ref[t + dt, start : start + 2 * W, 0 : 3 * C], w_down[dt * 3 + dr])
                total = part if total is None else total + part
        out_down[t] = total

    put_stats(3, 1, *join_stats(3, 0, stats, False))
    stats = send_stats(3, 1)
    sums_sd.third()
    sums_f.third()
    first, second = join_stats(3, 1, stats, False)
    mean_one, mean_two = over_group(first) * count, over_group(second) * count

    @pl.loop(0, T)
    def _(t):
        normed = (v_ext[t + 2, W : (R + 1) * W, :].astype(F32) - centre_one) * scale_one
        out_video[t] = g_block[t] + scale_one * (t1[t] - mean_one - normed * mean_two)

    sums_sd.finish()
    sums_f.finish()


def finish_kernel(down, video, sums_sd, sums_f, out_down, out_video, out_first, out_second, out_grad_down):
    for p in range(W):
        here = slice(p * L, (p + 1) * L)
        out_video[0, 0, :, here] = video[0, pl.ds(p, R, stride=W), :]
        out_down[0, 0, :, here] = down[0, pl.ds(p, 2, stride=W), :].astype(BF16)

    @pl.when(pl.program_id(0) == 0)
    def _():
        for source, target in ((sums_sd, out_second), (sums_f, out_first)):
            for tile in range(TILES):
                width = min(L, 27 * C - tile * L)
                value = source[tile * C : (tile + 1) * C, :].astype(F32)
                target[:, tile * L : tile * L + width] = value[:, 0:width]
        out_grad_down[...] = sums_sd[HALF : HALF + 27 * C, :].astype(F32)


def local(video, conv_first, conv_second, conv_down, down_cotangent):
    operands = (
        video, down_cotangent, conv_first.T, conv_second.T, conv_down.reshape(9, 3 * C, C_OUT)
    )
    rows = (R + 2) * W

    def reduction(piece):
        return [
            pltpu.VMEM((piece * PLANE, L), F32),
            pltpu.VMEM((piece * PLANE, L), BF16),
            pltpu.VMEM((PLANE - 1, piece, L), BF16),
            pltpu.VMEM((piece, L), BF16),
            pltpu.VMEM((COLUMN, piece, L), BF16),
        ]

    vmem = pl.BlockSpec(memory_space=pltpu.VMEM)
    dma = pltpu.SemaphoreType.DMA
    results = pl.pallas_call(
        kernel,
        out_shape=(
            jax.ShapeDtypeStruct((T, 2 * W, L), F32),
            jax.ShapeDtypeStruct((T, R * W, L), F32),
            jax.ShapeDtypeStruct((PIECE_SD * PLANE, L), BF16),
            jax.ShapeDtypeStruct((PIECE_F * PLANE, L), BF16),
        ),
        in_specs=[vmem] * len(operands),
        out_specs=(vmem,) * 4,
        scratch_shapes=[
            pltpu.VMEM((C, TILES * L), F32),
            pltpu.VMEM((4, 3, 4 * C, 4 * C), BF16),
            pltpu.VMEM((4, 3, 4 * C, 4 * C), BF16),
            pltpu.VMEM((4, 3, 4 * C, 4 * C), BF16),
            pltpu.VMEM((4, 3, 4 * C, 4 * C), BF16),
            pltpu.VMEM((9, 2 * C, 2 * C_OUT), BF16),
            pltpu.VMEM((T // 2 * R * W, 2 * L), F32),
            pltpu.VMEM((T + 2, rows, L), BF16),
            pltpu.VMEM((T, R * W, L), F32),
            pltpu.VMEM((2 * T, 4 * W, L), BF16),
            pltpu.VMEM((T, 2 * W, L), F32),
            pltpu.VMEM((2 * T, 4 * W, 2 * L), BF16),
            pltpu.VMEM((T, R * W, L), F32),
            pltpu.VMEM((T + 4, rows, L), BF16),
            pltpu.VMEM((T + 2, rows, L), BF16),
            pltpu.VMEM((T, R * W, L), F32),
            pltpu.VMEM((T, R * W, L), F32),
            pltpu.VMEM((T + 2, rows, 2 * L), BF16),
            pltpu.VMEM((T + 2, rows, 2 * L), BF16),
            pltpu.VMEM((T + 2, rows, 2 * L), BF16),
            pltpu.VMEM((T + 2, (R + 1) * W, L), BF16),
            pltpu.VMEM((T + 2, 3 * W, 2 * L), BF16),
            pltpu.VMEM((T + 2, 2 * W, 2 * L), BF16),
            pltpu.VMEM((L, CELLS), BF16),
            pltpu.VMEM((L, CELLS // 2), BF16),
            pltpu.VMEM((4, 2, 8, L), F32),
            pltpu.VMEM((4, 2, LOW, 8, L), F32),
            *reduction(PIECE_SD),
            *reduction(PIECE_F),
            dma((2, 20)),
            dma((2, 4, 2, LOW)),
            dma((2, 2, PLANE)),
            dma((2, 2, COLUMN)),
            dma((2, 2, PLANE)),
        ],
        compiler_params=pltpu.CompilerParams(
            collective_id=1, has_side_effects=True, vmem_limit_bytes=56 * 1024 * 1024
        ),
    )(*operands)

    def frame(*shape):
        return pl.BlockSpec(shape, lambda t: (t,) + (0,) * (len(shape) - 1))

    def out_frame(rows):
        return pl.BlockSpec((1, 1, rows, W * L), lambda t: (0, t, 0, 0))

    def whole(*shape):
        return pl.BlockSpec(shape, lambda t: (0,) * len(shape))

    down, grad_video, first, second, grad_down = pl.pallas_call(
        finish_kernel,
        grid=(T,),
        out_shape=(
            jax.ShapeDtypeStruct((1, T, 2, W * L), BF16),
            jax.ShapeDtypeStruct((1, T, R, W * L), F32),
            jax.ShapeDtypeStruct((C, 27 * C), F32),
            jax.ShapeDtypeStruct((C, 27 * C), F32),
            jax.ShapeDtypeStruct((27 * C, C_OUT), F32),
        ),
        in_specs=[
            frame(1, 2 * W, L),
            frame(1, R * W, L),
            whole(PIECE_SD * PLANE, L),
            whole(PIECE_F * PLANE, L),
        ],
        out_specs=(
            out_frame(2), out_frame(R), whole(C, 27 * C), whole(C, 27 * C), whole(27 * C, C_OUT)
        ),
        compiler_params=pltpu.CompilerParams(vmem_limit_bytes=60 * 1024 * 1024),
    )(*results)
    return down, grad_video, first.T, second.T, grad_down


def solution(mesh):
    in_specs = (P("clip", "tm", "space", None), P(), P(), P(), P("clip", "tm", "space", None))
    out_specs = (P("clip", "tm", "space", None), P("clip", "tm", "space", None), P(), P(), P())
    return jax.shard_map(local, mesh=mesh, in_specs=in_specs, out_specs=out_specs, check_vma=False)
```

```python
import functools
import math

import jax
import jax.numpy as jnp
from jax import lax
from jax.experimental import pallas as pl
from jax.experimental.pallas import tpu as pltpu
from jax.sharding import PartitionSpec as P

MESH = pl.DeviceIdType.MESH
F32 = jnp.float32
BF16 = jnp.bfloat16
EPSILON = 1e-06
C = 64
C_OUT = 128
T = 4
R = 4
W = 80
L = 128
TM = 32
LOW = 8
HIGH = 8
PLANE = 16
COLUMN = 8
PIECE_S = 64
PIECE_D = 128
PIECE_F = 64
TILES = 14
HALF = TILES * C
CELLS = T * R * W
GROUP_CELLS = CELLS * 64


def low_peer(step):
    tm = lax.axis_index("tm")
    low = lax.rem(tm, LOW)
    return {"tm": tm - low + lax.rem(low + step, LOW)}


def high_peer(step):
    tm, space = lax.axis_index("tm"), lax.axis_index("space")
    place = lax.rem((tm // LOW) * 2 + space + step, HIGH)
    return {"tm": (place // 2) * LOW + lax.rem(tm, LOW), "space": lax.rem(place, 2)}


def plane_place():
    return lax.axis_index("tm") // 2


def plane_peer(step):
    tm = lax.axis_index("tm")
    return {"tm": lax.rem(tm // 2 + step, PLANE) * 2 + lax.rem(tm, 2)}


def column_place():
    core = lax.rem(lax.axis_index("tm"), 2)
    return (core * 2 + lax.axis_index("space")) * 2 + lax.axis_index("clip")


def column_peer(step):
    tm = lax.axis_index("tm")
    place = lax.rem(column_place() + step, COLUMN)
    return {
        "tm": (tm // 2) * 2 + place // 4,
        "space": lax.rem(place // 2, 2),
        "clip": lax.rem(place, 2),
    }


def near(step, across):
    tm, space = lax.axis_index("tm"), lax.axis_index("space")
    device = {}
    if step:
        device["tm"] = lax.rem(tm + step + TM, TM)
    if across:
        device["space"] = 1 - space
    return device


def ends(copies):
    for copy in copies:
        copy.wait()


def begins(copies):
    for copy in copies:
        copy.start()
    return copies


def lanes(shape):
    return lax.broadcasted_iota(jnp.int32, shape, len(shape) - 1)


def over_group(value):
    wide = jnp.broadcast_to(value, (8, L))
    both = wide + pltpu.roll(wide, C, 1)
    even = lax.rem(lanes((8, L)), 2) == 0
    other = jnp.where(even, pltpu.roll(both, L - 1, 1), pltpu.roll(both, 1, 1))
    return (both + other)[0:1]


def put_windows(target, f, r, x):
    turned = pltpu.roll(x, C, 1)
    row = lax.broadcasted_iota(jnp.int32, (W, L), 0)
    left = lanes((W, L)) < C
    above = jnp.where(row == 0, 0.0, pltpu.roll(turned, 1, 0))
    below = jnp.where(row == W - 1, 0.0, pltpu.roll(turned, W - 1, 0))
    target[f, r * W : (r + 1) * W, 0:L] = jnp.where(left, above, turned).astype(BF16)
    target[f, r * W : (r + 1) * W, L : 2 * L] = jnp.where(left, turned, below).astype(BF16)


def dot_turned(a, b):
    return lax.dot_general(a, b, (((1,), (1,)), ((), ())), preferred_element_type=F32)


def dot(a, b):
    return jnp.dot(a, b, preferred_element_type=F32)


def conv(windows, weights, total, multiply):
    total[...] = jnp.zeros_like(total)

    @pl.loop(0, 4)
    def _(o):
        value = None
        for dr in range(3):
            rows = slice(dr * W, (dr + R) * W)
            both = jnp.concatenate([windows[o, rows, :], windows[o + 2, rows, :]], axis=0)
            part = multiply(both, weights[o, dr])
            value = part if value is None else value + part
        total[...] = total[...] + value


def put_kernels(raw, padded, ahead, back):
    width = 27 * C
    padded[:, 0:width] = raw[...].astype(F32)
    padded[:, width:] = jnp.zeros((C, padded.shape[1] - width), F32)
    lane = lanes((C, 4 * C))
    for dr in range(3):
        ahead[0, dr, 2 * C : 4 * C, :] = jnp.zeros((2 * C, 4 * C), BF16)
        ahead[3, dr, 0 : 2 * C, :] = jnp.zeros((2 * C, 4 * C), BF16)
        back[0, dr, :, 2 * C : 4 * C] = jnp.zeros((4 * C, 2 * C), BF16)
        back[3, dr, :, 0 : 2 * C] = jnp.zeros((4 * C, 2 * C), BF16)
    for tap in range(9):
        start = tap * 3 * C
        if tap % 2 == 0:
            near = jnp.where(lane < 3 * C, padded[:, start : start + 4 * C], 0.0)
            later = pltpu.roll(near, C, 1)
        else:
            later = jnp.where(lane < C, 0.0, padded[:, start - C : start + 3 * C])
            near = pltpu.roll(later, 3 * C, 1)
        near, later = near.astype(BF16), later.astype(BF16)
        dt, dr = tap // 3, tap % 3
        for frame in range(2):
            base = frame * 2 * C
            ahead[dt + frame, dr, base : base + C, :] = near
            ahead[dt + frame, dr, base + C : base + 2 * C, :] = later
            target = back.at[2 - dt + frame, 2 - dr]
            here = slice(base, base + 2 * C)
            target[0:C, here] = near[:, 2 * C :]
            target[C : 2 * C, here] = later[:, 2 * C :]
            target[2 * C : 3 * C, here] = near[:, 0 : 2 * C]
            target[3 * C : 4 * C, here] = later[:, 0 : 2 * C]


def sigmoid(value):
    return 0.5 + 0.5 * jnp.tanh(0.5 * value)


def transposed(source):
    return source.T.astype(BF16)


def kernel(
    video, cot, raw_first, raw_second, w_down,
    out_down, out_video, all_s, all_d, all_f,
    padded, w_first, w_second, b_first, b_second, b_down, wide,
    v_ext, field, c_ext, c_field, c_win, g_block, h_ext, t2_ext, t2, t1, win_first, win_second,
    win_back, b_ext, b_even, b_odd, gt, gtc, st_src, st_buf,
    full_s, send_s, recv_s, sum_s, recvb_s,
    full_d, send_d, recv_d, sum_d, recvb_d,
    full_f, send_f, recv_f, sum_f, recvb_f,
    halo_sems, st_sems, wa_sems, wb_sems, wc_sems, wd_sems,
):
    tm, space = lax.axis_index("tm"), lax.axis_index("space")
    low = lax.rem(tm, LOW)
    high = (tm // LOW) * 2 + space
    plane, column = plane_place(), column_place()
    core = lax.rem(tm, 2)
    has_past = jnp.where(tm == 0, 0.0, 1.0).astype(F32)
    has_next = jnp.where(tm == TM - 1, 0.0, 1.0).astype(F32)
    has_above = jnp.where(space == 0, 0.0, 1.0).astype(F32)
    has_below = jnp.where(space == 1, 0.0, 1.0).astype(F32)
    one = jnp.ones((), F32)

    def row_mask(r):
        return has_above if r == 0 else has_below if r == R + 1 else one

    edge = pl.multiple_of((R - (R - 1) * space) * W, W)
    far = pl.multiple_of((R + 1) * space * W, W)

    peers = [low_peer(k) for k in range(1, LOW)] + [high_peer(k) for k in range(1, HIGH)]
    peers += [plane_peer(k) for k in range(1, PLANE)] + [column_peer(k) for k in range(1, COLUMN)]
    peers += [near(1, False), near(-1, False), near(1, True), near(-1, True)]
    barrier = pltpu.get_barrier_semaphore()
    for peer in peers:
        pl.semaphore_signal(barrier, inc=1, device_id=peer, device_id_type=MESH)

    def remote(source, target, send, recv, device):
        return pltpu.make_async_remote_copy(
            src_ref=source, dst_ref=target, send_sem=send, recv_sem=recv,
            device_id=device, device_id_type=MESH,
        )

    def halo(slot, source, target, device):
        return remote(source, target, halo_sems.at[0, slot], halo_sems.at[1, slot], device)

    def send_stats(k, stage):
        me, peer, size = (high, high_peer, HIGH) if stage == 0 else (low, low_peer, LOW)
        copies = begins([
            remote(
                st_src.at[k, stage], st_buf.at[k, stage, me],
                st_sems.at[0, k, stage, j], st_sems.at[1, k, stage, j], peer(j),
            )
            for j in range(1, size)
        ])
        st_buf[k, stage, me] = st_src[k, stage]
        return copies

    def join_stats(k, stage, copies, centred):
        ends(copies)
        parts = [st_buf[k, stage, j] for j in range(LOW)]
        total = parts[0]
        for part in parts[1:]:
            total = total + part
        first, second = total[0:1], total[1:2]
        if centred:
            cells = float(CELLS * (1 if stage == 0 else LOW))
            first = first * (1.0 / LOW)
            for part in parts:
                second = second + cells * ((part[0:1] - first) * (part[0:1] - first))
        return first, second

    def put_stats(k, stage, first, second):
        st_src[k, stage] = jnp.zeros((8, L), F32)
        st_src[k, stage, 0:1] = first
        st_src[k, stage, 1:2] = second

    def scale_of(mean, spread):
        centre = over_group(mean) * 0.25
        gap = mean - centre
        variance = over_group(spread + float(GROUP_CELLS) * (gap * gap)) * (1.0 / (4 * GROUP_CELLS))
        return centre, lax.rsqrt(variance + EPSILON)

    def spread_of(mean, read):
        def step(t, total):
            gap = read(t) - mean
            return total + jnp.sum(gap * gap, axis=0, keepdims=True)

        return lax.fori_loop(0, T, step, jnp.zeros((1, L), F32))

    def take_video(t, total):
        for p in range(W):
            field[t, pl.ds(p, R, stride=W), :] = video[0, t, :, p * L : (p + 1) * L].astype(F32)
        value = field[t]
        v_ext[t + 2, W : (R + 1) * W, :] = value.astype(BF16)
        return total + jnp.sum(value, axis=0, keepdims=True)

    mean = lax.fori_loop(0, T, take_video, jnp.zeros((1, L), F32)) * (1.0 / CELLS)
    put_stats(0, 0, mean, spread_of(mean, lambda t: field[t]))
    pl.semaphore_wait(barrier, len(peers))
    stats = send_stats(0, 0)
    own = pl.ds(W, R * W)
    video_halo = begins([
        halo(0, v_ext.at[T : T + 2, own], v_ext.at[0:2, own], near(1, False)),
        halo(1, v_ext.at[2 : T + 2, pl.ds(edge, W)], v_ext.at[2 : T + 2, pl.ds(far, W)], near(0, True)),
        halo(2, v_ext.at[T : T + 2, pl.ds(edge, W)], v_ext.at[0:2, pl.ds(far, W)], near(1, True)),
    ])
    for ref in (v_ext, h_ext, t2_ext):
        for f in range(ref.shape[0]):
            ref[f, pl.ds(far, W), :] = jnp.zeros((W, L), ref.dtype)

    @pl.loop(0, T)
    def _(t):
        for p in range(W):
            c_field[t, pl.ds(p, 2, stride=W), :] = cot[0, t, :, p * L : (p + 1) * L].astype(F32)
        c_ext[t, W : 3 * W, :] = c_field[t].astype(BF16)

    c_own = pl.ds(W, 2 * W)
    c_edge = pl.ds(pl.multiple_of((2 - space) * W, W), W)
    c_far = pl.ds(pl.multiple_of(3 * space * W, W), W)
    cot_halo = begins([
        halo(3, c_ext.at[0:T, c_own], c_ext.at[T : 2 * T, c_own], near(-1, False)),
        halo(4, c_ext.at[0:T, c_edge], c_ext.at[0:T, c_far], near(0, True)),
        halo(5, c_ext.at[0:T, c_edge], c_ext.at[T : 2 * T, c_far], near(-1, True)),
    ])
    for f in range(2 * T):
        c_ext[f, c_far, :] = jnp.zeros((W, L), BF16)
    put_kernels(raw_first, padded, w_first, b_first)
    put_stats(0, 1, *join_stats(0, 0, stats, True))
    stats = send_stats(0, 1)
    for half in range(2):
        both = c_field[2 * half : 2 * half + 2].reshape(4 * W, L)
        gtc[:, half * 4 * W : half * 4 * W + 4 * W] = transposed(both)
    for tap in range(9):
        b_down[8 - tap, 0:C, 0:L] = w_down[tap, C : 2 * C, :]
        b_down[8 - tap, 0:C, L : 2 * L] = jnp.zeros((C, L), BF16)
        b_down[8 - tap, C : 2 * C, 0:L] = w_down[tap, 2 * C : 3 * C, :]
        b_down[8 - tap, C : 2 * C, L : 2 * L] = w_down[tap, 0:C, :]
    ends(cot_halo)

    @pl.loop(0, 2 * T)
    def _(f):
        late = jnp.where(f >= T, has_next, one)
        row = lax.broadcasted_iota(jnp.int32, (W, L), 0)
        for r in range(4):
            value = c_ext[f, r * W : (r + 1) * W, :].astype(F32)
            value = value * (late * has_above if r == 0 else late * has_below if r == 3 else late)
            after = jnp.where(row == W - 1, 0.0, pltpu.roll(value, W - 1, 0))
            c_win[f, r * W : (r + 1) * W, 0:L] = value.astype(BF16)
            c_win[f, r * W : (r + 1) * W, L : 2 * L] = after.astype(BF16)

    @pl.loop(0, T + 2)
    def _(f):
        late = jnp.where(f >= T, has_next, one)
        even = odd = None
        for j in range(3):
            upper = c_win[f + j, 0 : 3 * W, :]
            lower = c_win[f + j, W : 4 * W, :]
            a = dot_turned(lower, b_down[j * 3 + 1])
            b = dot_turned(upper, b_down[j * 3])
            b = b + dot_turned(lower, b_down[j * 3 + 2])
            even, odd = (a, b) if j == 0 else (even + a, odd + b)
        for i in range(3):
            for r, value in ((2 * i, odd), (2 * i + 1, even)):
                put_windows(win_back, f, r, value[i * W : (i + 1) * W] * (late * row_mask(r)))

        @pl.when(f < T)
        def _():
            for r in range(1, R + 1):
                value = (even if r % 2 else odd)[(r // 2) * W : (r // 2 + 1) * W]
                g_block[f, (r - 1) * W : r * W, :] = value

    centre_one, scale_one = scale_of(*join_stats(0, 1, stats, True))
    ends(video_halo)

    @pl.loop(0, T + 2)
    def _(f):
        early = jnp.where(f < 2, has_past, one)
        for r in range(R + 2):
            normed = (v_ext[f, r * W : (r + 1) * W, :].astype(F32) - centre_one) * scale_one
            put_windows(win_first, f, r, normed * sigmoid(normed) * (early * row_mask(r)))

    def result(q, frame):
        here = slice(frame * L, (frame + 1) * L)
        return wide[q * R * W : (q + 1) * R * W, here]

    def frames_of(step, start):
        for q in range(T // 2):
            for frame in range(2):
                start = step(2 * q + frame, result(q, frame), start)
        return start

    def first_conv(t, value, total):
        hidden = value.astype(BF16)
        h_ext[t + 2, W : (R + 1) * W, :] = hidden
        return total + jnp.sum(hidden.astype(F32), axis=0, keepdims=True)

    conv(win_first, w_first, wide, dot_turned)
    mean = frames_of(first_conv, jnp.zeros((1, L), F32)) * (1.0 / CELLS)

    def own_hidden(t):
        return h_ext[t + 2, W : (R + 1) * W, :].astype(F32)

    put_stats(1, 0, mean, spread_of(mean, own_hidden))
    stats = send_stats(1, 0)
    hidden_halo = begins([
        halo(9, h_ext.at[T : T + 2, own], h_ext.at[0:2, own], near(1, False)),
        halo(10, h_ext.at[2 : T + 2, pl.ds(edge, W)], h_ext.at[2 : T + 2, pl.ds(far, W)], near(0, True)),
        halo(11, h_ext.at[T : T + 2, pl.ds(edge, W)], h_ext.at[0:2, pl.ds(far, W)], near(1, True)),
        halo(12, h_ext.at[2:4, own], h_ext.at[T + 2 : T + 4, own], near(-1, False)),
        halo(13, h_ext.at[2:4, pl.ds(edge, W)], h_ext.at[T + 2 : T + 4, pl.ds(far, W)], near(-1, True)),
    ])

    put_kernels(raw_second, padded, w_second, b_second)
    for half in range(2):
        both = g_block[2 * half : 2 * half + 2].reshape(8 * W, L)
        gt[:, half * 8 * W : (half + 1) * 8 * W] = transposed(both)

    put_stats(1, 1, *join_stats(1, 0, stats, True))
    stats = send_stats(1, 1)

    def keep_back(t, value, _):
        t2[t] = value
        t2_ext[t, W : (R + 1) * W, :] = value.astype(BF16)

    conv(win_back, b_second, wide, dot)
    frames_of(keep_back, None)

    act_halo = begins([
        halo(14, t2_ext.at[0:2, own], t2_ext.at[T : T + 2, own], near(-1, False)),
        halo(15, t2_ext.at[0:T, pl.ds(edge, W)], t2_ext.at[0:T, pl.ds(far, W)], near(0, True)),
        halo(16, t2_ext.at[0:2, pl.ds(edge, W)], t2_ext.at[T : T + 2, pl.ds(far, W)], near(-1, True)),
    ])

    centre_two, scale_two = scale_of(*join_stats(1, 1, stats, True))

    def gradient(grad, normed):
        sigma = sigmoid(normed)
        return grad * sigma * (1.0 + normed * (1.0 - sigma))

    def second_sums(t, sums):
        first, second = sums
        for r in range(1, R + 1):
            normed = (h_ext[t + 2, r * W : (r + 1) * W, :].astype(F32) - centre_two) * scale_two
            grad = gradient(t2[t, (r - 1) * W : r * W, :], normed)
            t2[t, (r - 1) * W : r * W, :] = grad
            first = first + jnp.sum(grad, axis=0, keepdims=True)
            second = second + jnp.sum(grad * normed, axis=0, keepdims=True)
        return first, second

    nothing = (jnp.zeros((1, L), F32), jnp.zeros((1, L), F32))
    put_stats(2, 0, *lax.fori_loop(0, T, second_sums, nothing))
    stats = send_stats(2, 0)
    ends(hidden_halo)

    @pl.loop(0, T + 2)
    def _(f):
        early = jnp.where(f < 2, has_past, one)
        for r in range(R + 2):
            normed = (h_ext[f, r * W : (r + 1) * W, :].astype(F32) - centre_two) * scale_two
            put_windows(win_second, f, r, normed * sigmoid(normed) * (early * row_mask(r)))

    put_stats(2, 1, *join_stats(2, 0, stats, False))
    stats = send_stats(2, 1)

    def add_input(t, value, _):
        block = v_ext[t + 2, W : (R + 1) * W, :].astype(F32) + value
        b_ext[t + 2, W : (R + 1) * W, :] = block.astype(BF16)

    conv(win_second, w_second, wide, dot_turned)
    frames_of(add_input, None)

    block_halo = begins([
        halo(17, b_ext.at[T : T + 2, own], b_ext.at[0:2, own], near(1, False)),
        halo(18, b_ext.at[2 : T + 2, pl.ds(R * W, W)], b_ext.at[2 : T + 2, pl.ds(0, W)], near(0, True)),
        halo(19, b_ext.at[T : T + 2, pl.ds(R * W, W)], b_ext.at[0:2, pl.ds(0, W)], near(1, True)),
    ])

    class Reduction:
        def __init__(self, number, piece, full, send, recv, sums, recvb, whole):
            self.n, self.half = number, piece // 2
            self.full, self.send, self.recv, self.sums = full, send, recv, sums
            self.recvb, self.whole = recvb, whole

        def sem(self, sems, *k):
            return sems.at[(0, self.n) + k], sems.at[(1, self.n) + k]

        def start(self):
            self.send[...] = self.full[...].reshape(self.send.shape).astype(BF16)
            self.copies = begins([
                remote(
                    self.send.at[:, lax.rem(plane + k, PLANE)], self.recv.at[k - 1],
                    *self.sem(wa_sems, k), plane_peer(k),
                )
                for k in range(1, PLANE)
            ])

        def second(self):
            ends(self.copies)
            for h in range(2):
                row = pl.multiple_of((h * PLANE + plane) * self.half, 16)
                value = self.full[pl.ds(row, self.half), :]
                for k in range(PLANE - 1):
                    value = value + self.recv[k, h].astype(F32)
                self.sums[h] = value.astype(BF16)
            self.copies = begins([
                remote(
                    self.sums.at[lax.rem(column + k, COLUMN) // 4], self.recvb.at[column],
                    *self.sem(wb_sems, k), column_peer(k),
                )
                for k in range(1, COLUMN)
            ])
            self.recvb[column] = self.sums[core]

        def third(self):
            ends(self.copies)
            value = self.recvb[0].astype(F32)
            for k in range(1, COLUMN):
                value = value + self.recvb[k].astype(F32)
            value = value * (1.0 / math.sqrt(2 * 128 * 8 * 160))
            self.whole[core, plane] = value.astype(BF16)
            here = self.whole.at[core, plane]
            self.copies = begins([
                remote(here, here, *self.sem(wc_sems, k), plane_peer(k)) for k in range(1, PLANE)
            ])

        def fourth(self):
            ends(self.copies)
            here = self.whole.at[core]
            self.copies = begins([remote(here, here, *self.sem(wd_sems), {"tm": tm + 1 - 2 * core})])

        def finish(self):
            ends(self.copies)

    sums_s = Reduction(0, PIECE_S, full_s, send_s, recv_s, sum_s, recvb_s, all_s)
    sums_d = Reduction(1, PIECE_D, full_d, send_d, recv_d, sum_d, recvb_d, all_d)
    sums_f = Reduction(2, PIECE_F, full_f, send_f, recv_f, sum_f, recvb_f, all_f)

    def block_weights(windows, full):
        left = lanes((C, L)) < C

        def folded(tap):
            dt, dr = tap // 3, tap % 3
            cells = windows[dt : dt + T, dr * W : (dr + R) * W, :].reshape(CELLS, 2 * L)
            both = dot(gt[...], cells)
            return both[0:C] + pltpu.roll(both[C : 2 * C], 3 * C, 1)

        def put(tile, value):
            full[tile * C : (tile + 1) * C, :] = value

        for pair in range(4):
            a, b = folded(2 * pair), pltpu.roll(folded(2 * pair + 1), C, 1)
            put(3 * pair, a[:, 0:L])
            put(3 * pair + 1, jnp.where(left, a[:, L : 2 * L], b[:, 0:L]))
            put(3 * pair + 2, b[:, L : 2 * L])
        value = folded(8)
        put(12, value[:, 0:L])
        put(13, jnp.where(left, value[:, L : 2 * L], 0.0))

    full_s[HALF:, :] = jnp.zeros((full_s.shape[0] - HALF, L), F32)
    full_d[27 * C :, :] = jnp.zeros((full_d.shape[0] - 27 * C, L), F32)
    full_f[HALF:, :] = jnp.zeros((full_f.shape[0] - HALF, L), F32)
    block_weights(win_second, full_s)
    sums_s.start()

    ends(block_halo)

    @pl.loop(0, T + 2)
    def _(f):
        early = jnp.where(f < 2, has_past, one)
        for r in range(R + 1):
            value = b_ext[f, r * W : (r + 1) * W, :].astype(F32) * (early * has_above if r == 0 else early)
            put_windows(b_odd if r % 2 else b_even, f, r // 2, value)

    def projected(dr):
        return (b_even, 0) if dr == 0 else (b_odd, 0) if dr == 1 else (b_even, W)

    for dt in range(3):
        for dr in range(3):
            ref, start = projected(dr)
            cells = ref[dt : dt + T, start : start + 2 * W, :].reshape(2 * W * T, 2 * L)
            turned = jnp.dot(gtc[...], cells, preferred_element_type=F32).T
            base = (dt * 3 + dr) * 3 * C
            full_d[base : base + 3 * C, :] = turned[0 : 3 * C]
    sums_d.start()


    count = 1.0 / (4 * GROUP_CELLS)
    first, second = join_stats(2, 1, stats, False)
    mean_one, mean_two = over_group(first) * count, over_group(second) * count

    def hidden_row(f, r, normed, grad, mask):
        hidden = scale_two * (grad - mean_one - normed * mean_two)
        put_windows(win_back, f, r, hidden * mask)
        return hidden

    def second_normed(f, r):
        return (h_ext[f + 2, r * W : (r + 1) * W, :].astype(F32) - centre_two) * scale_two

    def far_row(f, r, mask):
        normed = second_normed(f, r)
        grad = gradient(t2_ext[f, r * W : (r + 1) * W, :].astype(F32), normed)
        hidden_row(f, r, normed, grad, mask)

    @pl.loop(0, T)
    def _(f):
        for r in range(1, R + 1):
            here = slice((r - 1) * W, r * W)
            field[f, here, :] = hidden_row(f, r, second_normed(f, r), t2[f, here, :], one)

    for half in range(2):
        both = field[2 * half : 2 * half + 2].reshape(8 * W, L)
        gt[:, half * 8 * W : (half + 1) * 8 * W] = transposed(both)
    block_weights(win_first, full_f)
    sums_f.start()
    sums_s.second()
    ends(act_halo)

    @pl.loop(0, T)
    def _(f):
        for r in (0, R + 1):
            far_row(f, r, row_mask(r))

    @pl.loop(T, T + 2)
    def _(f):
        for r in range(R + 2):
            far_row(f, r, has_next * row_mask(r))

    sums_d.second()

    def back_first(t, back, sums):
        normed = (v_ext[t + 2, W : (R + 1) * W, :].astype(F32) - centre_one) * scale_one
        grad = gradient(back, normed)
        t1[t] = grad
        return (
            sums[0] + jnp.sum(grad, axis=0, keepdims=True),
            sums[1] + jnp.sum(grad * normed, axis=0, keepdims=True),
        )

    conv(win_back, b_first, wide, dot)
    put_stats(3, 0, *frames_of(back_first, nothing))
    stats = send_stats(3, 0)
    sums_s.third()
    sums_f.second()

    @pl.loop(0, T)
    def _(t):
        total = None
        for dt in range(3):
            for dr in range(3):
                ref, start = projected(dr)
                part = dot(ref[t + dt, start : start + 2 * W, 0 : 3 * C], w_down[dt * 3 + dr])
                total = part if total is None else total + part
        out_down[t] = total

    sums_d.third()
    put_stats(3, 1, *join_stats(3, 0, stats, False))
    stats = send_stats(3, 1)
    sums_f.third()
    first, second = join_stats(3, 1, stats, False)
    mean_one, mean_two = over_group(first) * count, over_group(second) * count

    @pl.loop(0, T)
    def _(t):
        normed = (v_ext[t + 2, W : (R + 1) * W, :].astype(F32) - centre_one) * scale_one
        out_video[t] = g_block[t] + scale_one * (t1[t] - mean_one - normed * mean_two)

    for sums in (sums_s, sums_d, sums_f):
        sums.fourth()
    for sums in (sums_s, sums_d, sums_f):
        sums.finish()


def finish_kernel(down, video, sums_s, sums_d, sums_f, out_down, out_video, out_first, out_second, out_grad_down):
    for p in range(W):
        here = slice(p * L, (p + 1) * L)
        out_video[0, 0, :, here] = video[0, pl.ds(p, R, stride=W), :]
        out_down[0, 0, :, here] = down[0, pl.ds(p, 2, stride=W), :].astype(BF16)

    for source, target in ((sums_s, out_second), (sums_f, out_first)):
        for tile in range(PLANE // T):
            value = source[tile * C : (tile + 1) * C, :].astype(F32)
            target[:, tile * L : (tile + 1) * L] = value
    out_grad_down[...] = sums_d[...].astype(F32)


def local(video, conv_first, conv_second, conv_down, down_cotangent):
    operands = (
        video, down_cotangent, conv_first.T, conv_second.T, conv_down.reshape(9, 3 * C, C_OUT)
    )
    rows = (R + 2) * W

    def reduction(piece):
        half = (2, piece // 2, L)
        return [
            pltpu.VMEM((piece * PLANE, L), F32),
            pltpu.VMEM((2, PLANE, piece // 2, L), BF16),
            pltpu.VMEM((PLANE - 1,) + half, BF16),
            pltpu.VMEM(half, BF16),
            pltpu.VMEM((COLUMN,) + half[1:], BF16),
        ]

    vmem = pl.BlockSpec(memory_space=pltpu.VMEM)
    dma = pltpu.SemaphoreType.DMA
    results = pl.pallas_call(
        kernel,
        out_shape=(
            jax.ShapeDtypeStruct((T, 2 * W, L), F32),
            jax.ShapeDtypeStruct((T, R * W, L), F32),
            *(
                jax.ShapeDtypeStruct((2, PLANE, piece // 2, L), BF16)
                for piece in (PIECE_S, PIECE_D, PIECE_F)
            ),
        ),
        in_specs=[vmem] * len(operands),
        out_specs=(vmem,) * 5,
        scratch_shapes=[
            pltpu.VMEM((C, TILES * L), F32),
            pltpu.VMEM((4, 3, 4 * C, 4 * C), BF16),
            pltpu.VMEM((4, 3, 4 * C, 4 * C), BF16),
            pltpu.VMEM((4, 3, 4 * C, 4 * C), BF16),
            pltpu.VMEM((4, 3, 4 * C, 4 * C), BF16),
            pltpu.VMEM((9, 2 * C, 2 * C_OUT), BF16),
            pltpu.VMEM((T // 2 * R * W, 2 * L), F32),
            pltpu.VMEM((T + 2, rows, L), BF16),
            pltpu.VMEM((T, R * W, L), F32),
            pltpu.VMEM((2 * T, 4 * W, L), BF16),
            pltpu.VMEM((T, 2 * W, L), F32),
            pltpu.VMEM((2 * T, 4 * W, 2 * L), BF16),
            pltpu.VMEM((T, R * W, L), F32),
            pltpu.VMEM((T + 4, rows, L), BF16),
            pltpu.VMEM((T + 2, rows, L), BF16),
            pltpu.VMEM((T, R * W, L), F32),
            pltpu.VMEM((T, R * W, L), F32),
            pltpu.VMEM((T + 2, rows, 2 * L), BF16),
            pltpu.VMEM((T + 2, rows, 2 * L), BF16),
            pltpu.VMEM((T + 2, rows, 2 * L), BF16),
            pltpu.VMEM((T + 2, (R + 1) * W, L), BF16),
            pltpu.VMEM((T + 2, 3 * W, 2 * L), BF16),
            pltpu.VMEM((T + 2, 2 * W, 2 * L), BF16),
            pltpu.VMEM((L, CELLS), BF16),
            pltpu.VMEM((L, CELLS // 2), BF16),
            pltpu.VMEM((4, 2, 8, L), F32),
            pltpu.VMEM((4, 2, LOW, 8, L), F32),
            *reduction(PIECE_S),
            *reduction(PIECE_D),
            *reduction(PIECE_F),
            dma((2, 20)),
            dma((2, 4, 2, LOW)),
            dma((2, 3, PLANE)),
            dma((2, 3, COLUMN)),
            dma((2, 3, PLANE)),
            dma((2, 3)),
        ],
        compiler_params=pltpu.CompilerParams(
            collective_id=1, has_side_effects=True, vmem_limit_bytes=56 * 1024 * 1024
        ),
    )(*operands)

    def frame(*shape):
        return pl.BlockSpec(shape, lambda t: (t,) + (0,) * (len(shape) - 1))

    def out_frame(rows):
        return pl.BlockSpec((1, 1, rows, W * L), lambda t: (0, t, 0, 0))

    down, grad_video, first, second, grad_down = pl.pallas_call(
        finish_kernel,
        grid=(T,),
        out_shape=(
            jax.ShapeDtypeStruct((1, T, 2, W * L), BF16),
            jax.ShapeDtypeStruct((1, T, R, W * L), F32),
            jax.ShapeDtypeStruct((C, 27 * C), F32),
            jax.ShapeDtypeStruct((C, 27 * C), F32),
            jax.ShapeDtypeStruct((27 * C, C_OUT), F32),
        ),
        in_specs=[
            frame(1, 2 * W, L),
            frame(1, R * W, L),
            frame(PIECE_S * PLANE // T, L),
            frame(27 * C // T, L),
            frame(PIECE_F * PLANE // T, L),
        ],
        out_specs=(
            out_frame(2),
            out_frame(R),
            pl.BlockSpec((C, PLANE // T * L), lambda t: (0, t)),
            pl.BlockSpec((C, PLANE // T * L), lambda t: (0, t)),
            frame(27 * C // T, C_OUT),
        ),
        compiler_params=pltpu.CompilerParams(vmem_limit_bytes=60 * 1024 * 1024),
    )(*results[:2], *(sums.reshape(-1, L) for sums in results[2:]))
    return down, grad_video, first.T, second.T, grad_down


def solution(mesh):
    in_specs = (P("clip", "tm", "space", None), P(), P(), P(), P("clip", "tm", "space", None))
    out_specs = (P("clip", "tm", "space", None), P("clip", "tm", "space", None), P(), P(), P())
    return jax.shard_map(local, mesh=mesh, in_specs=in_specs, out_specs=out_specs, check_vma=False)
```

```python
import functools
import math

import jax
import jax.numpy as jnp
from jax import lax
from jax.experimental import pallas as pl
from jax.experimental.pallas import tpu as pltpu
from jax.sharding import PartitionSpec as P

MESH = pl.DeviceIdType.MESH
F32 = jnp.float32
BF16 = jnp.bfloat16
EPSILON = 1e-06
C = 64
C_OUT = 128
T = 4
R = 4
W = 80
L = 128
TM = 32
LOW = 8
HIGH = 8
PLANE = 16
COLUMN = 8
PIECE_S = 64
PIECE_D = 128
PIECE_F = 64
TILES = 14
HALF = TILES * C
CELLS = T * R * W
GROUP_CELLS = CELLS * 64


def low_peer(step):
    tm = lax.axis_index("tm")
    low = lax.rem(tm, LOW)
    return {"tm": tm - low + lax.rem(low + step, LOW)}


def high_peer(step):
    tm, space = lax.axis_index("tm"), lax.axis_index("space")
    place = lax.rem((tm // LOW) * 2 + space + step, HIGH)
    return {"tm": (place // 2) * LOW + lax.rem(tm, LOW), "space": lax.rem(place, 2)}


def plane_place():
    return lax.axis_index("tm") // 2


def plane_peer(step):
    tm = lax.axis_index("tm")
    return {"tm": lax.rem(tm // 2 + step, PLANE) * 2 + lax.rem(tm, 2)}


def column_place():
    core = lax.rem(lax.axis_index("tm"), 2)
    return (core * 2 + lax.axis_index("space")) * 2 + lax.axis_index("clip")


def column_peer(step):
    tm = lax.axis_index("tm")
    place = lax.rem(column_place() + step, COLUMN)
    return {
        "tm": (tm // 2) * 2 + place // 4,
        "space": lax.rem(place // 2, 2),
        "clip": lax.rem(place, 2),
    }


def near(step, across):
    tm, space = lax.axis_index("tm"), lax.axis_index("space")
    device = {}
    if step:
        device["tm"] = lax.rem(tm + step + TM, TM)
    if across:
        device["space"] = 1 - space
    return device


def ends(copies):
    for copy in copies:
        copy.wait()


def begins(copies):
    for copy in copies:
        copy.start()
    return copies


def lanes(shape):
    return lax.broadcasted_iota(jnp.int32, shape, len(shape) - 1)


def over_group(value):
    wide = jnp.broadcast_to(value, (8, L))
    both = wide + pltpu.roll(wide, C, 1)
    even = lax.rem(lanes((8, L)), 2) == 0
    other = jnp.where(even, pltpu.roll(both, L - 1, 1), pltpu.roll(both, 1, 1))
    return (both + other)[0:1]


def put_windows(target, f, r, x):
    turned = pltpu.roll(x, C, 1)
    row = lax.broadcasted_iota(jnp.int32, (W, L), 0)
    left = lanes((W, L)) < C
    above = jnp.where(row == 0, 0.0, pltpu.roll(turned, 1, 0))
    below = jnp.where(row == W - 1, 0.0, pltpu.roll(turned, W - 1, 0))
    target[f, r * W : (r + 1) * W, 0:L] = jnp.where(left, above, turned).astype(BF16)
    target[f, r * W : (r + 1) * W, L : 2 * L] = jnp.where(left, turned, below).astype(BF16)


def dot_turned(a, b):
    return lax.dot_general(a, b, (((1,), (1,)), ((), ())), preferred_element_type=F32)


def dot(a, b):
    return jnp.dot(a, b, preferred_element_type=F32)


def conv(windows, weights, total, multiply):
    total[...] = jnp.zeros_like(total)

    @pl.loop(0, 4)
    def _(o):
        value = None
        for dr in range(3):
            rows = slice(dr * W, (dr + R) * W)
            both = jnp.concatenate([windows[o, rows, :], windows[o + 2, rows, :]], axis=0)
            part = multiply(both, weights[o, dr])
            value = part if value is None else value + part
        total[...] = total[...] + value


def put_kernels(raw, padded, ahead, back):
    width = 27 * C
    padded[:, 0:width] = raw[...].astype(F32)
    padded[:, width:] = jnp.zeros((C, padded.shape[1] - width), F32)
    lane = lanes((C, 4 * C))
    for dr in range(3):
        ahead[0, dr, 2 * C : 4 * C, :] = jnp.zeros((2 * C, 4 * C), BF16)
        ahead[3, dr, 0 : 2 * C, :] = jnp.zeros((2 * C, 4 * C), BF16)
        back[0, dr, :, 2 * C : 4 * C] = jnp.zeros((4 * C, 2 * C), BF16)
        back[3, dr, :, 0 : 2 * C] = jnp.zeros((4 * C, 2 * C), BF16)
    for tap in range(9):
        start = tap * 3 * C
        if tap % 2 == 0:
            near = jnp.where(lane < 3 * C, padded[:, start : start + 4 * C], 0.0)
            later = pltpu.roll(near, C, 1)
        else:
            later = jnp.where(lane < C, 0.0, padded[:, start - C : start + 3 * C])
            near = pltpu.roll(later, 3 * C, 1)
        near, later = near.astype(BF16), later.astype(BF16)
        dt, dr = tap // 3, tap % 3
        for frame in range(2):
            base = frame * 2 * C
            ahead[dt + frame, dr, base : base + C, :] = near
            ahead[dt + frame, dr, base + C : base + 2 * C, :] = later
            target = back.at[2 - dt + frame, 2 - dr]
            here = slice(base, base + 2 * C)
            target[0:C, here] = near[:, 2 * C :]
            target[C : 2 * C, here] = later[:, 2 * C :]
            target[2 * C : 3 * C, here] = near[:, 0 : 2 * C]
            target[3 * C : 4 * C, here] = later[:, 0 : 2 * C]


def sigmoid(value):
    return 0.5 + 0.5 * jnp.tanh(0.5 * value)


def transposed(source):
    return source.T.astype(BF16)


def kernel(
    video, cot, raw_first, raw_second, w_down,
    out_down, out_video, all_s, all_d, all_f,
    padded, w_first, w_second, b_first, b_second, b_down, wide,
    v_ext, field, c_ext, c_field, c_win, g_block, h_ext, t2_ext, t2, t1, win_first, win_second,
    win_back, b_ext, b_even, b_odd, gt, gtc, st_src, st_buf,
    full_s, send_s, recv_s, sum_s, recvb_s,
    full_d, send_d, recv_d, sum_d, recvb_d,
    full_f, send_f, recv_f, sum_f, recvb_f,
    halo_sems, st_sems, wa_sems, wb_sems, wc_sems, wd_sems,
):
    tm, space = lax.axis_index("tm"), lax.axis_index("space")
    low = lax.rem(tm, LOW)
    high = (tm // LOW) * 2 + space
    plane, column = plane_place(), column_place()
    core = lax.rem(tm, 2)
    has_past = jnp.where(tm == 0, 0.0, 1.0).astype(F32)
    has_next = jnp.where(tm == TM - 1, 0.0, 1.0).astype(F32)
    has_above = jnp.where(space == 0, 0.0, 1.0).astype(F32)
    has_below = jnp.where(space == 1, 0.0, 1.0).astype(F32)
    one = jnp.ones((), F32)

    def row_mask(r):
        return has_above if r == 0 else has_below if r == R + 1 else one

    edge = pl.multiple_of((R - (R - 1) * space) * W, W)
    far = pl.multiple_of((R + 1) * space * W, W)

    peers = [low_peer(k) for k in range(1, LOW)] + [high_peer(k) for k in range(1, HIGH)]
    peers += [plane_peer(k) for k in range(1, PLANE)] + [column_peer(k) for k in range(1, COLUMN)]
    peers += [near(1, False), near(-1, False), near(1, True), near(-1, True)]
    barrier = pltpu.get_barrier_semaphore()
    for peer in peers:
        pl.semaphore_signal(barrier, inc=1, device_id=peer, device_id_type=MESH)

    def remote(source, target, send, recv, device):
        return pltpu.make_async_remote_copy(
            src_ref=source, dst_ref=target, send_sem=send, recv_sem=recv,
            device_id=device, device_id_type=MESH,
        )

    def halo(slot, source, target, device):
        return remote(source, target, halo_sems.at[0, slot], halo_sems.at[1, slot], device)

    def send_stats(k, stage):
        me, peer, size = (high, high_peer, HIGH) if stage == 0 else (low, low_peer, LOW)
        copies = begins([
            remote(
                st_src.at[k, stage], st_buf.at[k, stage, me],
                st_sems.at[0, k, stage, j], st_sems.at[1, k, stage, j], peer(j),
            )
            for j in range(1, size)
        ])
        st_buf[k, stage, me] = st_src[k, stage]
        return copies

    def join_stats(k, stage, copies, centred):
        ends(copies)
        parts = [st_buf[k, stage, j] for j in range(LOW)]
        total = parts[0]
        for part in parts[1:]:
            total = total + part
        first, second = total[0:1], total[1:2]
        if centred:
            cells = float(CELLS * (1 if stage == 0 else LOW))
            first = first * (1.0 / LOW)
            for part in parts:
                second = second + cells * ((part[0:1] - first) * (part[0:1] - first))
        return first, second

    def put_stats(k, stage, first, second):
        st_src[k, stage] = jnp.zeros((8, L), F32)
        st_src[k, stage, 0:1] = first
        st_src[k, stage, 1:2] = second

    def scale_of(mean, spread):
        centre = over_group(mean) * 0.25
        gap = mean - centre
        variance = over_group(spread + float(GROUP_CELLS) * (gap * gap)) * (1.0 / (4 * GROUP_CELLS))
        return centre, lax.rsqrt(variance + EPSILON)

    def spread_of(mean, read):
        def step(t, total):
            gap = read(t) - mean
            return total + jnp.sum(gap * gap, axis=0, keepdims=True)

        return lax.fori_loop(0, T, step, jnp.zeros((1, L), F32))

    def take_video(t, total):
        for p in range(W):
            field[t, pl.ds(p, R, stride=W), :] = video[0, t, :, p * L : (p + 1) * L].astype(F32)
        value = field[t]
        v_ext[t + 2, W : (R + 1) * W, :] = value.astype(BF16)
        return total + jnp.sum(value, axis=0, keepdims=True)

    mean = lax.fori_loop(0, T, take_video, jnp.zeros((1, L), F32)) * (1.0 / CELLS)
    put_stats(0, 0, mean, spread_of(mean, lambda t: field[t]))
    pl.semaphore_wait(barrier, len(peers))
    stats = send_stats(0, 0)
    own = pl.ds(W, R * W)
    video_halo = begins([
        halo(0, v_ext.at[T : T + 2, own], v_ext.at[0:2, own], near(1, False)),
        halo(1, v_ext.at[2 : T + 2, pl.ds(edge, W)], v_ext.at[2 : T + 2, pl.ds(far, W)], near(0, True)),
        halo(2, v_ext.at[T : T + 2, pl.ds(edge, W)], v_ext.at[0:2, pl.ds(far, W)], near(1, True)),
    ])
    for ref in (v_ext, h_ext, t2_ext):
        for f in range(ref.shape[0]):
            ref[f, pl.ds(far, W), :] = jnp.zeros((W, L), ref.dtype)

    @pl.loop(0, T)
    def _(t):
        for p in range(W):
            c_field[t, pl.ds(p, 2, stride=W), :] = cot[0, t, :, p * L : (p + 1) * L].astype(F32)
        c_ext[t, W : 3 * W, :] = c_field[t].astype(BF16)

    c_own = pl.ds(W, 2 * W)
    c_edge = pl.ds(pl.multiple_of((2 - space) * W, W), W)
    c_far = pl.ds(pl.multiple_of(3 * space * W, W), W)
    cot_halo = begins([
        halo(3, c_ext.at[0:T, c_own], c_ext.at[T : 2 * T, c_own], near(-1, False)),
        halo(4, c_ext.at[0:T, c_edge], c_ext.at[0:T, c_far], near(0, True)),
        halo(5, c_ext.at[0:T, c_edge], c_ext.at[T : 2 * T, c_far], near(-1, True)),
    ])
    for f in range(2 * T):
        c_ext[f, c_far, :] = jnp.zeros((W, L), BF16)
    put_kernels(raw_first, padded, w_first, b_first)
    put_stats(0, 1, *join_stats(0, 0, stats, True))
    stats = send_stats(0, 1)
    for half in range(2):
        both = c_field[2 * half : 2 * half + 2].reshape(4 * W, L)
        gtc[:, half * 4 * W : half * 4 * W + 4 * W] = transposed(both)
    for tap in range(9):
        b_down[8 - tap, 0:C, 0:L] = w_down[tap, C : 2 * C, :]
        b_down[8 - tap, 0:C, L : 2 * L] = jnp.zeros((C, L), BF16)
        b_down[8 - tap, C : 2 * C, 0:L] = w_down[tap, 2 * C : 3 * C, :]
        b_down[8 - tap, C : 2 * C, L : 2 * L] = w_down[tap, 0:C, :]
    ends(cot_halo)

    @pl.loop(0, 2 * T)
    def _(f):
        late = jnp.where(f >= T, has_next, one)
        row = lax.broadcasted_iota(jnp.int32, (W, L), 0)
        for r in range(4):
            value = c_ext[f, r * W : (r + 1) * W, :].astype(F32)
            value = value * (late * has_above if r == 0 else late * has_below if r == 3 else late)
            after = jnp.where(row == W - 1, 0.0, pltpu.roll(value, W - 1, 0))
            c_win[f, r * W : (r + 1) * W, 0:L] = value.astype(BF16)
            c_win[f, r * W : (r + 1) * W, L : 2 * L] = after.astype(BF16)

    @pl.loop(0, T + 2)
    def _(f):
        late = jnp.where(f >= T, has_next, one)
        even = odd = None
        for j in range(3):
            upper = c_win[f + j, 0 : 3 * W, :]
            lower = c_win[f + j, W : 4 * W, :]
            a = dot_turned(lower, b_down[j * 3 + 1])
            b = dot_turned(upper, b_down[j * 3])
            b = b + dot_turned(lower, b_down[j * 3 + 2])
            even, odd = (a, b) if j == 0 else (even + a, odd + b)
        for i in range(3):
            for r, value in ((2 * i, odd), (2 * i + 1, even)):
                put_windows(win_back, f, r, value[i * W : (i + 1) * W] * (late * row_mask(r)))

        @pl.when(f < T)
        def _():
            for r in range(1, R + 1):
                value = (even if r % 2 else odd)[(r // 2) * W : (r // 2 + 1) * W]
                g_block[f, (r - 1) * W : r * W, :] = value

    centre_one, scale_one = scale_of(*join_stats(0, 1, stats, True))
    ends(video_halo)

    @pl.loop(0, T + 2)
    def _(f):
        early = jnp.where(f < 2, has_past, one)
        for r in range(R + 2):
            normed = (v_ext[f, r * W : (r + 1) * W, :].astype(F32) - centre_one) * scale_one
            put_windows(win_first, f, r, normed * sigmoid(normed) * (early * row_mask(r)))

    def result(q, frame):
        here = slice(frame * L, (frame + 1) * L)
        return wide[q * R * W : (q + 1) * R * W, here]

    def frames_of(step, start):
        for q in range(T // 2):
            for frame in range(2):
                start = step(2 * q + frame, result(q, frame), start)
        return start

    def first_conv(t, value, total):
        hidden = value.astype(BF16)
        h_ext[t + 2, W : (R + 1) * W, :] = hidden
        return total + jnp.sum(hidden.astype(F32), axis=0, keepdims=True)

    conv(win_first, w_first, wide, dot_turned)
    mean = frames_of(first_conv, jnp.zeros((1, L), F32)) * (1.0 / CELLS)

    def own_hidden(t):
        return h_ext[t + 2, W : (R + 1) * W, :].astype(F32)

    put_stats(1, 0, mean, spread_of(mean, own_hidden))
    stats = send_stats(1, 0)
    hidden_halo = begins([
        halo(9, h_ext.at[T : T + 2, own], h_ext.at[0:2, own], near(1, False)),
        halo(10, h_ext.at[2 : T + 2, pl.ds(edge, W)], h_ext.at[2 : T + 2, pl.ds(far, W)], near(0, True)),
        halo(11, h_ext.at[T : T + 2, pl.ds(edge, W)], h_ext.at[0:2, pl.ds(far, W)], near(1, True)),
        halo(12, h_ext.at[2:4, own], h_ext.at[T + 2 : T + 4, own], near(-1, False)),
        halo(13, h_ext.at[2:4, pl.ds(edge, W)], h_ext.at[T + 2 : T + 4, pl.ds(far, W)], near(-1, True)),
    ])

    put_kernels(raw_second, padded, w_second, b_second)
    for half in range(2):
        both = g_block[2 * half : 2 * half + 2].reshape(8 * W, L)
        gt[:, half * 8 * W : (half + 1) * 8 * W] = transposed(both)

    put_stats(1, 1, *join_stats(1, 0, stats, True))
    stats = send_stats(1, 1)

    def keep_back(t, value, _):
        t2[t] = value
        t2_ext[t, W : (R + 1) * W, :] = value.astype(BF16)

    conv(win_back, b_second, wide, dot)
    frames_of(keep_back, None)

    act_halo = begins([
        halo(14, t2_ext.at[0:2, own], t2_ext.at[T : T + 2, own], near(-1, False)),
        halo(15, t2_ext.at[0:T, pl.ds(edge, W)], t2_ext.at[0:T, pl.ds(far, W)], near(0, True)),
        halo(16, t2_ext.at[0:2, pl.ds(edge, W)], t2_ext.at[T : T + 2, pl.ds(far, W)], near(-1, True)),
    ])

    centre_two, scale_two = scale_of(*join_stats(1, 1, stats, True))

    def gradient(grad, normed):
        sigma = sigmoid(normed)
        return grad * sigma * (1.0 + normed * (1.0 - sigma))

    def second_sums(t, sums):
        first, second = sums
        for r in range(1, R + 1):
            normed = (h_ext[t + 2, r * W : (r + 1) * W, :].astype(F32) - centre_two) * scale_two
            grad = gradient(t2[t, (r - 1) * W : r * W, :], normed)
            t2[t, (r - 1) * W : r * W, :] = grad
            first = first + jnp.sum(grad, axis=0, keepdims=True)
            second = second + jnp.sum(grad * normed, axis=0, keepdims=True)
        return first, second

    nothing = (jnp.zeros((1, L), F32), jnp.zeros((1, L), F32))
    put_stats(2, 0, *lax.fori_loop(0, T, second_sums, nothing))
    stats = send_stats(2, 0)
    ends(hidden_halo)

    @pl.loop(0, T + 2)
    def _(f):
        early = jnp.where(f < 2, has_past, one)
        for r in range(R + 2):
            normed = (h_ext[f, r * W : (r + 1) * W, :].astype(F32) - centre_two) * scale_two
            put_windows(win_second, f, r, normed * sigmoid(normed) * (early * row_mask(r)))

    put_stats(2, 1, *join_stats(2, 0, stats, False))
    stats = send_stats(2, 1)

    def add_input(t, value, _):
        block = v_ext[t + 2, W : (R + 1) * W, :].astype(F32) + value
        b_ext[t + 2, W : (R + 1) * W, :] = block.astype(BF16)

    conv(win_second, w_second, wide, dot_turned)
    frames_of(add_input, None)

    block_halo = begins([
        halo(17, b_ext.at[T : T + 2, own], b_ext.at[0:2, own], near(1, False)),
        halo(18, b_ext.at[2 : T + 2, pl.ds(R * W, W)], b_ext.at[2 : T + 2, pl.ds(0, W)], near(0, True)),
        halo(19, b_ext.at[T : T + 2, pl.ds(R * W, W)], b_ext.at[0:2, pl.ds(0, W)], near(1, True)),
    ])

    class Reduction:
        def __init__(self, number, piece, full, send, recv, sums, recvb, whole):
            self.n, self.half = number, piece // 2
            self.full, self.send, self.recv, self.sums = full, send, recv, sums
            self.recvb, self.whole = recvb, whole

        def sem(self, sems, *k):
            return sems.at[(0, self.n) + k], sems.at[(1, self.n) + k]

        def start(self):
            self.send[...] = self.full[...].reshape(self.send.shape).astype(BF16)
            self.copies = begins([
                remote(
                    self.send.at[:, lax.rem(plane + k, PLANE)], self.recv.at[k - 1],
                    *self.sem(wa_sems, k), plane_peer(k),
                )
                for k in range(1, PLANE)
            ])

        def second(self):
            ends(self.copies)
            for h in range(2):
                row = pl.multiple_of((h * PLANE + plane) * self.half, 16)
                value = self.full[pl.ds(row, self.half), :]
                for k in range(PLANE - 1):
                    value = value + self.recv[k, h].astype(F32)
                self.sums[h] = value.astype(BF16)
            self.copies = begins([
                remote(
                    self.sums.at[lax.rem(column + k, COLUMN) // 4], self.recvb.at[column],
                    *self.sem(wb_sems, k), column_peer(k),
                )
                for k in range(1, COLUMN)
            ])
            self.recvb[column] = self.sums[core]

        def third(self):
            ends(self.copies)
            value = self.recvb[0].astype(F32)
            for k in range(1, COLUMN):
                value = value + self.recvb[k].astype(F32)
            value = value * (1.0 / math.sqrt(2 * 128 * 8 * 160))
            self.whole[core, plane] = value.astype(BF16)
            here = self.whole.at[core, plane]
            self.copies = begins([
                remote(here, here, *self.sem(wc_sems, k), plane_peer(k)) for k in range(1, PLANE)
            ])

        def fourth(self):
            ends(self.copies)
            here = self.whole.at[core]
            self.copies = begins([remote(here, here, *self.sem(wd_sems), {"tm": tm + 1 - 2 * core})])

        def finish(self):
            ends(self.copies)

    sums_s = Reduction(0, PIECE_S, full_s, send_s, recv_s, sum_s, recvb_s, all_s)
    sums_d = Reduction(1, PIECE_D, full_d, send_d, recv_d, sum_d, recvb_d, all_d)
    sums_f = Reduction(2, PIECE_F, full_f, send_f, recv_f, sum_f, recvb_f, all_f)

    def block_weights(windows, full):
        left = lanes((C, L)) < C

        def folded(tap):
            dt, dr = tap // 3, tap % 3
            cells = windows[dt : dt + T, dr * W : (dr + R) * W, :].reshape(CELLS, 2 * L)
            both = dot(gt[...], cells)
            return both[0:C] + pltpu.roll(both[C : 2 * C], 3 * C, 1)

        def put(tile, value):
            full[tile * C : (tile + 1) * C, :] = value

        for pair in range(4):
            a, b = folded(2 * pair), pltpu.roll(folded(2 * pair + 1), C, 1)
            put(3 * pair, a[:, 0:L])
            put(3 * pair + 1, jnp.where(left, a[:, L : 2 * L], b[:, 0:L]))
            put(3 * pair + 2, b[:, L : 2 * L])
        value = folded(8)
        put(12, value[:, 0:L])
        put(13, jnp.where(left, value[:, L : 2 * L], 0.0))

    full_s[HALF:, :] = jnp.zeros((full_s.shape[0] - HALF, L), F32)
    full_d[27 * C :, :] = jnp.zeros((full_d.shape[0] - 27 * C, L), F32)
    full_f[HALF:, :] = jnp.zeros((full_f.shape[0] - HALF, L), F32)
    block_weights(win_second, full_s)
    sums_s.start()

    ends(block_halo)

    @pl.loop(0, T + 2)
    def _(f):
        early = jnp.where(f < 2, has_past, one)
        for r in range(R + 1):
            value = b_ext[f, r * W : (r + 1) * W, :].astype(F32) * (early * has_above if r == 0 else early)
            put_windows(b_odd if r % 2 else b_even, f, r // 2, value)

    def projected(dr):
        return (b_even, 0) if dr == 0 else (b_odd, 0) if dr == 1 else (b_even, W)

    for dt in range(3):
        for dr in range(3):
            ref, start = projected(dr)
            cells = ref[dt : dt + T, start : start + 2 * W, :].reshape(2 * W * T, 2 * L)
            turned = jnp.dot(gtc[...], cells, preferred_element_type=F32).T
            base = (dt * 3 + dr) * 3 * C
            full_d[base : base + 3 * C, :] = turned[0 : 3 * C]
    sums_d.start()


    count = 1.0 / (4 * GROUP_CELLS)
    first, second = join_stats(2, 1, stats, False)
    mean_one, mean_two = over_group(first) * count, over_group(second) * count

    def hidden_row(f, r, normed, grad, mask):
        hidden = scale_two * (grad - mean_one - normed * mean_two)
        put_windows(win_back, f, r, hidden * mask)
        return hidden

    def second_normed(f, r):
        return (h_ext[f + 2, r * W : (r + 1) * W, :].astype(F32) - centre_two) * scale_two

    def far_row(f, r, mask):
        normed = second_normed(f, r)
        grad = gradient(t2_ext[f, r * W : (r + 1) * W, :].astype(F32), normed)
        hidden_row(f, r, normed, grad, mask)

    @pl.loop(0, T)
    def _(f):
        for r in range(1, R + 1):
            here = slice((r - 1) * W, r * W)
            field[f, here, :] = hidden_row(f, r, second_normed(f, r), t2[f, here, :], one)

    for half in range(2):
        both = field[2 * half : 2 * half + 2].reshape(8 * W, L)
        gt[:, half * 8 * W : (half + 1) * 8 * W] = transposed(both)
    block_weights(win_first, full_f)
    sums_f.start()
    sums_s.second()
    ends(act_halo)

    @pl.loop(0, T)
    def _(f):
        for r in (0, R + 1):
            far_row(f, r, row_mask(r))

    @pl.loop(T, T + 2)
    def _(f):
        for r in range(R + 2):
            far_row(f, r, has_next * row_mask(r))

    sums_d.second()

    def back_first(t, back, sums):
        normed = (v_ext[t + 2, W : (R + 1) * W, :].astype(F32) - centre_one) * scale_one
        grad = gradient(back, normed)
        t1[t] = grad
        return (
            sums[0] + jnp.sum(grad, axis=0, keepdims=True),
            sums[1] + jnp.sum(grad * normed, axis=0, keepdims=True),
        )

    conv(win_back, b_first, wide, dot)
    sums_f.second()
    put_stats(3, 0, *frames_of(back_first, nothing))
    stats = send_stats(3, 0)
    sums_s.third()

    @pl.loop(0, T)
    def _(t):
        total = None
        for dt in range(3):
            for dr in range(3):
                ref, start = projected(dr)
                part = dot(ref[t + dt, start : start + 2 * W, 0 : 3 * C], w_down[dt * 3 + dr])
                total = part if total is None else total + part
        out_down[t] = total

    sums_d.third()
    put_stats(3, 1, *join_stats(3, 0, stats, False))
    stats = send_stats(3, 1)
    sums_f.third()
    first, second = join_stats(3, 1, stats, False)
    mean_one, mean_two = over_group(first) * count, over_group(second) * count

    @pl.loop(0, T)
    def _(t):
        normed = (v_ext[t + 2, W : (R + 1) * W, :].astype(F32) - centre_one) * scale_one
        out_video[t] = g_block[t] + scale_one * (t1[t] - mean_one - normed * mean_two)

    for sums in (sums_s, sums_d, sums_f):
        sums.fourth()
    for sums in (sums_s, sums_d, sums_f):
        sums.finish()


def finish_kernel(down, video, sums_s, sums_d, sums_f, out_down, out_video, out_first, out_second, out_grad_down):
    for p in range(W):
        here = slice(p * L, (p + 1) * L)
        out_video[0, 0, :, here] = video[0, pl.ds(p, R, stride=W), :]
        out_down[0, 0, :, here] = down[0, pl.ds(p, 2, stride=W), :].astype(BF16)

    for source, target in ((sums_s, out_second), (sums_f, out_first)):
        for tile in range(PLANE // T):
            value = source[tile * C : (tile + 1) * C, :].astype(F32)
            target[:, tile * L : (tile + 1) * L] = value
    out_grad_down[...] = sums_d[...].astype(F32)


def local(video, conv_first, conv_second, conv_down, down_cotangent):
    operands = (
        video, down_cotangent, conv_first.T, conv_second.T, conv_down.reshape(9, 3 * C, C_OUT)
    )
    rows = (R + 2) * W

    def reduction(piece):
        half = (2, piece // 2, L)
        return [
            pltpu.VMEM((piece * PLANE, L), F32),
            pltpu.VMEM((2, PLANE, piece // 2, L), BF16),
            pltpu.VMEM((PLANE - 1,) + half, BF16),
            pltpu.VMEM(half, BF16),
            pltpu.VMEM((COLUMN,) + half[1:], BF16),
        ]

    vmem = pl.BlockSpec(memory_space=pltpu.VMEM)
    dma = pltpu.SemaphoreType.DMA
    results = pl.pallas_call(
        kernel,
        out_shape=(
            jax.ShapeDtypeStruct((T, 2 * W, L), F32),
            jax.ShapeDtypeStruct((T, R * W, L), F32),
            *(
                jax.ShapeDtypeStruct((2, PLANE, piece // 2, L), BF16)
                for piece in (PIECE_S, PIECE_D, PIECE_F)
            ),
        ),
        in_specs=[vmem] * len(operands),
        out_specs=(vmem,) * 5,
        scratch_shapes=[
            pltpu.VMEM((C, TILES * L), F32),
            pltpu.VMEM((4, 3, 4 * C, 4 * C), BF16),
            pltpu.VMEM((4, 3, 4 * C, 4 * C), BF16),
            pltpu.VMEM((4, 3, 4 * C, 4 * C), BF16),
            pltpu.VMEM((4, 3, 4 * C, 4 * C), BF16),
            pltpu.VMEM((9, 2 * C, 2 * C_OUT), BF16),
            pltpu.VMEM((T // 2 * R * W, 2 * L), F32),
            pltpu.VMEM((T + 2, rows, L), BF16),
            pltpu.VMEM((T, R * W, L), F32),
            pltpu.VMEM((2 * T, 4 * W, L), BF16),
            pltpu.VMEM((T, 2 * W, L), F32),
            pltpu.VMEM((2 * T, 4 * W, 2 * L), BF16),
            pltpu.VMEM((T, R * W, L), F32),
            pltpu.VMEM((T + 4, rows, L), BF16),
            pltpu.VMEM((T + 2, rows, L), BF16),
            pltpu.VMEM((T, R * W, L), F32),
            pltpu.VMEM((T, R * W, L), F32),
            pltpu.VMEM((T + 2, rows, 2 * L), BF16),
            pltpu.VMEM((T + 2, rows, 2 * L), BF16),
            pltpu.VMEM((T + 2, rows, 2 * L), BF16),
            pltpu.VMEM((T + 2, (R + 1) * W, L), BF16),
            pltpu.VMEM((T + 2, 3 * W, 2 * L), BF16),
            pltpu.VMEM((T + 2, 2 * W, 2 * L), BF16),
            pltpu.VMEM((L, CELLS), BF16),
            pltpu.VMEM((L, CELLS // 2), BF16),
            pltpu.VMEM((4, 2, 8, L), F32),
            pltpu.VMEM((4, 2, LOW, 8, L), F32),
            *reduction(PIECE_S),
            *reduction(PIECE_D),
            *reduction(PIECE_F),
            dma((2, 20)),
            dma((2, 4, 2, LOW)),
            dma((2, 3, PLANE)),
            dma((2, 3, COLUMN)),
            dma((2, 3, PLANE)),
            dma((2, 3)),
        ],
        compiler_params=pltpu.CompilerParams(
            collective_id=1, has_side_effects=True, vmem_limit_bytes=56 * 1024 * 1024
        ),
    )(*operands)

    def frame(*shape):
        return pl.BlockSpec(shape, lambda t: (t,) + (0,) * (len(shape) - 1))

    def out_frame(rows):
        return pl.BlockSpec((1, 1, rows, W * L), lambda t: (0, t, 0, 0))

    down, grad_video, first, second, grad_down = pl.pallas_call(
        finish_kernel,
        grid=(T,),
        out_shape=(
            jax.ShapeDtypeStruct((1, T, 2, W * L), BF16),
            jax.ShapeDtypeStruct((1, T, R, W * L), F32),
            jax.ShapeDtypeStruct((C, 27 * C), F32),
            jax.ShapeDtypeStruct((C, 27 * C), F32),
            jax.ShapeDtypeStruct((27 * C, C_OUT), F32),
        ),
        in_specs=[
            frame(1, 2 * W, L),
            frame(1, R * W, L),
            frame(PIECE_S * PLANE // T, L),
            frame(27 * C // T, L),
            frame(PIECE_F * PLANE // T, L),
        ],
        out_specs=(
            out_frame(2),
            out_frame(R),
            pl.BlockSpec((C, PLANE // T * L), lambda t: (0, t)),
            pl.BlockSpec((C, PLANE // T * L), lambda t: (0, t)),
            frame(27 * C // T, C_OUT),
        ),
        compiler_params=pltpu.CompilerParams(vmem_limit_bytes=60 * 1024 * 1024),
    )(*results[:2], *(sums.reshape(-1, L) for sums in results[2:]))
    return down, grad_video, first.T, second.T, grad_down


def solution(mesh):
    in_specs = (P("clip", "tm", "space", None), P(), P(), P(), P("clip", "tm", "space", None))
    out_specs = (P("clip", "tm", "space", None), P("clip", "tm", "space", None), P(), P(), P())
    return jax.shard_map(local, mesh=mesh, in_specs=in_specs, out_specs=out_specs, check_vma=False)
```
